256 devices in a mesh: side: 2 (over y_hi), slab: 128 (over x, y_lo, z, core).
Axes of the slice: x: 4, y: 4 (y_hi: 2, y_lo: 2; y = y_hi * 2 + y_lo), z: 8, core: 2. Of those that a mesh axis runs over, the one named last changes fastest.
Arguments:
- velocity: float32 [2, 4096, 4096], P('side', 'slab'), may hold values from -6 to 6
- kernel: bfloat16 [2, 9, 4096, 4096], P('side', None, 'slab'), may hold values from -4 to 4
- history: bfloat16 [2, 8, 2, 4096, 4096], P('side', None, None, 'slab'), may hold values from -24576 to 24576
- impedance: float32 [2], replicated, may hold values from 0.5 to 1.5
- prestress: float32 [4096, 4096], P('slab'), may hold values from 1 to 3
- strength: float32 [4096, 4096], P('slab'), may hold values from 0.5 to 2
- fault_state: float32 [4096, 4096], P('slab'), may hold values from -1 to 1
Outputs:
- new_velocity: float32 [2, 4096, 4096], P('side', 'slab')
- slip_rate: float32 [4096, 4096], P('slab')
- new_state: float32 [4096, 4096], P('slab')
The draws below stay inside these ranges and needn't reach their ends.
All inputs are finite; a program needn't handle non-finite values.
Results may differ from the reference program's by a relative error of at most 0.00058.
Values sent between devices are 32-bit elements; how exact they have to be, the bound alone decides.
A program may use at most 128 MiB of HBM per device.

```python
import math
import jax
import jax.numpy as jnp

NX = 4096
NZ = 4096
LAGS = 8
NEWTON = 4
STEPS = 2


def level_of(key, dims, split, least, high):
    loudness, own = 1.0, jax.random.fold_in(key, 6)
    for position, parts in split:
        heights = jnp.exp(jax.random.uniform(jax.random.fold_in(own, position), (parts,), jnp.float32, least / len(split), high / len(split)))
        loudness = loudness * jnp.repeat(heights, dims[position] // parts).reshape([-1 if axis == position else 1 for axis in range(len(dims))])
    return loudness


def normal_values(key, extent, width, bound, shards=(), held_as=jnp.bfloat16):
    entries = jax.random.normal(key, extent, jnp.float32) * width
    if len(shards) > 0:
        entries = level_of(key, extent, shards, -0.22, 0.18) * entries
    return jnp.clip(entries, min=-bound, max=bound).astype(held_as)


def setup_inputs(seed: int = 0) -> dict:
    splits = jax.random.split(jax.random.key(seed), 8)
    velocity = normal_values(splits[0], (2, NX, NZ), 1.0, 6.0, ((0, 2), (1, 128)), jnp.float32)
    kernel = normal_values(splits[1], (2, LAGS + 1, NZ, NX), 0.3, 4.0, ((0, 2), (2, 128)))
    history = normal_values(splits[2], (2, LAGS, 2, NZ, NX), NX, 24576.0, ((0, 2), (3, 128)))
    impedance = jnp.clip(jax.random.uniform(splits[3], (2,), jnp.float32, 0.5, 1.5), 0.5, 1.5)
    prestress = jnp.clip(1.0 + 2.0 * jax.random.uniform(splits[4], (NX, NZ), jnp.float32) ** level_of(splits[4], (NX, NZ), ((0, 128),), -0.2, 0.2), 1.0, 3.0)
    strength = jnp.clip(jnp.exp(math.log(2.0) - 1.3862944 * jax.random.uniform(splits[5], (NX, NZ), jnp.float32) ** level_of(splits[5], (NX, NZ), ((0, 128),), -0.2, 0.2)), 0.5, 2.0)
    fault_state = jnp.clip(jax.random.uniform(splits[6], (NX, NZ), jnp.float32, -1.0, 1.0) * level_of(splits[6], (NX, NZ), ((0, 128),), -0.4, 0.0), -1.0, 1.0)
    return dict(velocity=velocity, kernel=kernel, history=history, impedance=impedance, prestress=prestress, strength=strength, fault_state=fault_state)


def inverse_sinh(value):
    magnitude = jnp.abs(value)
    result = jnp.log1p(magnitude + magnitude * magnitude / (1.0 + jnp.sqrt(1.0 + magnitude * magnitude)))
    return jnp.where(value < 0.0, -result, result)

def forward_spectrum(field):
    spec = jnp.fft.fft2(field).T
    return jnp.stack([jnp.real(spec), jnp.imag(spec)]).astype(jnp.bfloat16)

def inverse_force(total):
    combined = total[0] + 1j * total[1]
    return jnp.real(jnp.fft.ifft2(combined.T))

def reference(velocity, kernel, history, impedance, prestress, strength, fault_state):
    eta_first = impedance[0]
    eta_second = impedance[1]
    eta_total = eta_first + eta_second
    weight_first = eta_second / eta_total
    weight_second = eta_first / eta_total
    eta_joint = eta_first * eta_second / eta_total
    speeds = [velocity[0], velocity[1]]
    lag_lists = [[history[0, lag] for lag in range(LAGS)], [history[1, lag] for lag in range(LAGS)]]
    state_now = fault_state
    rate = jnp.zeros_like(prestress)
    for step_index in range(STEPS):
        forces = []
        for side_index in range(2):
            spec = forward_spectrum(speeds[side_index])
            total = kernel[side_index, 0].astype(jnp.float32) * spec.astype(jnp.float32)
            for lag in range(LAGS):
                total = total + kernel[side_index, lag + 1].astype(jnp.float32) * lag_lists[side_index][lag].astype(jnp.float32)
            forces.append(inverse_force(total))
            lag_lists[side_index] = [spec] + lag_lists[side_index][:-1]
        coupled = weight_first * forces[0] + weight_second * forces[1]
        locked = prestress + coupled
        rate = locked / (eta_joint + strength)
        factor = 0.5 * jnp.exp(state_now)
        for iteration in range(NEWTON):
            scaled = factor * rate
            misfit = strength * inverse_sinh(scaled) + eta_joint * rate - locked
            slope = strength * factor / jnp.sqrt(1.0 + scaled * scaled) + eta_joint
            rate = rate - 0.5 * misfit / slope
        stress = locked - eta_joint * rate
        speeds = [(prestress + forces[0] - stress) / eta_first, -1.0 * (prestress + forces[1] - stress) / eta_second]
        state_now = state_now + 0.25 * (jnp.exp(-state_now) - jnp.abs(rate))
    return (jnp.stack(speeds), rate, state_now)
```

```python
import functools
import math

import jax
import jax.numpy as jnp
import ml_dtypes
import numpy as np
from jax import lax
from jax.experimental import pallas as pl
from jax.experimental.pallas import tpu as pltpu
from jax.sharding import PartitionSpec as P

NX = 4096
NZ = 4096
LAGS = 8
NEWTON = 4
STEPS = 2
SLABS = 128
ROWS = 32
LANES = 128
MESH = pl.DeviceIdType.MESH
F32 = jnp.float32
BF16 = jnp.bfloat16
VMEM_BYTES = 56 * 2**20


def high_low(table, axis):
    table = table.astype(np.float32)
    high = table.astype(ml_dtypes.bfloat16)
    low = (table - high.astype(np.float32)).astype(ml_dtypes.bfloat16)
    return np.concatenate([high, low, high], axis=axis)


def complex_matrix(count, sign):
    angle = 2.0 * math.pi / count * (np.outer(np.arange(count), np.arange(count)) % count)
    cos, sin = np.cos(angle), sign * np.sin(angle)
    return np.block([[cos, -sin], [sin, cos]])


def tables():
    forward, inverse = complex_matrix(128, -1.0), complex_matrix(128, 1.0)
    forward_32 = complex_matrix(32, -1.0).reshape(2, 32, 2, 32)
    inverse_32 = complex_matrix(32, 1.0).reshape(2, 32, 2, 32)
    eye = np.eye(8)
    z_first = np.einsum("ajn,xy->ajxny", forward_32[:, :, 0], eye).reshape(512, 256)
    x_second = np.einsum("akcgx,ij->akicgjx", forward_32.reshape(2, 32, 2, 4, 8), eye).reshape(512, 512)
    x_third = np.einsum("axck,ij->axickj", inverse_32, eye).reshape(512, 512)
    z_last = np.einsum("zcgj,xy->zxcgyj", inverse_32[0].reshape(32, 2, 4, 8), eye).reshape(256, 512) / (NX * NZ)
    phase = 2.0 * math.pi / 4096 * np.outer(np.arange(32), np.arange(128))
    twiddle = np.stack([np.cos(phase), np.sin(phase)]).astype(np.float32)
    return dict(
        z_first=high_low(z_first, 1),
        x_second=high_low(x_second, 1),
        x_third=high_low(x_third, 1),
        z_last=high_low(z_last, 1),
        forward_left=high_low(forward, 1),
        inverse_left=high_low(inverse, 1),
        forward_right=high_low(forward.T, 0),
        inverse_right=high_low(inverse.T, 0),
        twiddle=twiddle,
        twiddle_rows=np.repeat(twiddle, 8, axis=1),
    )


def split(value):
    high = value.astype(BF16)
    low = (value - high.astype(F32)).astype(BF16)
    return high, low


def left_product(table, value):
    high, low = split(value)
    stacked = jnp.concatenate([high, high, low], axis=0)
    return jnp.dot(table, stacked, preferred_element_type=F32)


def right_product(value, table):
    high, low = split(value)
    stacked = jnp.concatenate([high, high, low], axis=1)
    return jnp.dot(stacked, table, preferred_element_type=F32)


def left_product_transposed(table, value):
    high, low = split(value)
    stacked = jnp.concatenate([high, high, low], axis=1)
    return lax.dot_general(table, stacked, (((1,), (1,)), ((), ())), preferred_element_type=F32)


def turn(real, imag, cos, sin):
    return real * cos - imag * sin, real * sin + imag * cos


def put_group(ref, group, value):
    for part in range(2):
        for half in range(2):
            piece = value[part * 128 : part * 128 + 128, half * 128 : half * 128 + 128]
            ref[pl.ds(part * 8 + group * 2 + half, SLABS, stride=16), :] = piece


def get_group(ref, group):
    return jnp.concatenate(
        [
            jnp.concatenate(
                [ref[pl.ds(part * 8 + group * 2 + half, SLABS, stride=16), :] for half in range(2)], axis=1
            )
            for part in range(2)
        ],
        axis=0,
    )


def z_forward(field, send, t):
    cos, sin = t["twiddle_rows"][0], t["twiddle_rows"][1]
    for pair in range(2):
        columns = [
            jnp.concatenate(
                [field[group * 8 : group * 8 + 8, n * 128 : n * 128 + 128] for n in range(32)], axis=0
            )
            for group in (2 * pair, 2 * pair + 1)
        ]
        first = left_product(t["z_first"][...], jnp.concatenate(columns, axis=1))
        for q in range(2):
            piece = first[:, q * 128 : q * 128 + 128]
            real, imag = turn(piece[:256], piece[256:], cos, -sin)
            turned = jnp.concatenate([real, imag], axis=1)
            put_group(send, 2 * pair + q, left_product_transposed(t["forward_left"][...], turned))


def gather_stage(received, table, twiddle, sign, middle):
    for group in range(4):
        rows = get_group(received, group).T
        first = right_product(rows, table[...])
        cos = twiddle[0, group * 8 : group * 8 + 8, :][None]
        sin = sign * twiddle[1, group * 8 : group * 8 + 8, :][None]
        real, imag = turn(first[:, :128].reshape(32, 8, 128), first[:, 128:].reshape(32, 8, 128), cos, sin)
        middle[0, group] = real.reshape(256, 128)
        middle[1, group] = imag.reshape(256, 128)


def middle_columns(middle, pair):
    return jnp.concatenate(
        [
            jnp.concatenate(
                [middle[c, g, q * 64 : q * 64 + 64, :] for c in range(2) for g in range(4)], axis=0
            )
            for q in (2 * pair, 2 * pair + 1)
        ],
        axis=1,
    )


def spectrum_phase(step, received, kernel, history, spec, send, t, middle, wide):
    gather_stage(received, t["forward_right"], t["twiddle"], -1.0, middle)
    cos, sin = t["twiddle_rows"][0], t["twiddle_rows"][1]
    for pair in range(2):
        wide[...] = left_product(t["x_second"][...], middle_columns(middle, pair))

        def convolve(k, carry):
            lanes = pl.ds(pl.multiple_of(k * 128, 128), 128)
            rows = slice(pair * 16, pair * 16 + 16)
            weights = [kernel[lag, rows, lanes].astype(F32) for lag in range(LAGS + 1)]
            for part in range(2):
                place = pl.ds(pl.multiple_of(part * 256 + k * 8, 8), 8)
                fresh = wide[place, :]
                rounded = jnp.concatenate([fresh[:, :128], fresh[:, 128:]], axis=0).astype(BF16)
                total = weights[0] * rounded.astype(F32)
                for lag in range(LAGS):
                    if lag < step:
                        past = spec[part, rows, lanes]
                    else:
                        past = history[lag - step, part, rows, lanes]
                    total = total + weights[lag + 1] * past.astype(F32)
                if step == 0:
                    spec[part, rows, lanes] = rounded
                wide[place, :] = jnp.concatenate([total[:8], total[8:]], axis=1)
            return carry

        lax.fori_loop(0, 32, convolve, 0)
        third = left_product(t["x_third"][...], wide[...])
        for q in range(2):
            piece = third[:, q * 128 : q * 128 + 128]
            real, imag = turn(piece[:256], piece[256:], cos, sin)
            turned = jnp.concatenate([real, imag], axis=1)
            put_group(send, 2 * pair + q, left_product_transposed(t["inverse_left"][...], turned))


def z_inverse(received, force, t, middle):
    gather_stage(received, t["inverse_right"], t["twiddle"], 1.0, middle)
    for pair in range(2):
        last = left_product(t["z_last"][...], middle_columns(middle, pair))
        for q in range(2):
            group = 2 * pair + q
            for n in range(32):
                force[group * 8 : group * 8 + 8, n * 128 : n * 128 + 128] = last[
                    n * 8 : n * 8 + 8, q * 128 : q * 128 + 128
                ]


def friction(is_first, impedance, force, other, prestress, strength, state, speed, rate_out, state_out):
    eta_first, eta_second = impedance[0], impedance[1]
    eta_total = eta_first + eta_second
    weight_first = eta_second / eta_total
    weight_second = eta_first / eta_total
    eta_joint = eta_first * eta_second / eta_total
    own_weight = jnp.where(is_first, weight_first, weight_second)
    other_weight = jnp.where(is_first, weight_second, weight_first)
    own_scale = jnp.where(is_first, 1.0 / eta_first, -1.0 / eta_second)

    def solve(index, carry):
        row = pl.multiple_of(lax.rem(index, 4) * 8, 8)
        lane = pl.multiple_of(lax.div(index, 4) * 512, 512)
        at = (pl.ds(row, 8), pl.ds(lane, 512))
        own = force[at]
        stress_now = prestress[at]
        normal = strength[at]
        psi = state[at]
        locked = stress_now + (own_weight * own + other_weight * other[at])
        rate = locked / (eta_joint + normal)
        factor = 0.5 * jnp.exp(psi)
        normal_factor = normal * factor
        for _ in range(NEWTON):
            scaled = factor * rate
            magnitude = jnp.abs(scaled)
            square = magnitude * magnitude
            root = jnp.sqrt(1.0 + square)
            arc = jnp.log1p(magnitude + square / (1.0 + root))
            arc = jnp.where(scaled < 0.0, -arc, arc)
            misfit = normal * arc + eta_joint * rate - locked
            slope = normal_factor / root + eta_joint
            rate = rate - 0.5 * misfit / slope
        stress = locked - eta_joint * rate
        speed[at] = (stress_now + own - stress) * own_scale
        rate_out[at] = rate
        state_out[at] = psi + 0.25 * (jnp.exp(-psi) - jnp.abs(rate))
        return carry

    lax.fori_loop(0, 32, solve, 0)


def exchange(s_ref, r_ref, send_sem, recv_sem, own_sem):
    me = lax.axis_index("slab")
    side = lax.axis_index("side")
    barrier = pltpu.get_barrier_semaphore()

    def greet(i, carry):
        there = lax.rem(me + i, SLABS)
        pl.semaphore_signal(barrier, inc=1, device_id=(side, there), device_id_type=MESH)
        return carry

    lax.fori_loop(1, SLABS, greet, 0)
    own = pltpu.make_async_copy(s_ref.at[me], r_ref.at[me], own_sem)
    own.start()
    pl.semaphore_wait(barrier, SLABS - 1)

    def start(i, carry):
        there = lax.rem(me + i, SLABS)
        pltpu.make_async_remote_copy(
            src_ref=s_ref.at[there],
            dst_ref=r_ref.at[me],
            send_sem=send_sem,
            recv_sem=recv_sem,
            device_id=(side, there),
            device_id_type=MESH,
        ).start()
        return carry

    lax.fori_loop(1, SLABS, start, 0)
    own.wait()
    bulk = r_ref.at[pl.ds(0, SLABS - 1)]
    pltpu.make_async_copy(bulk, bulk, recv_sem).wait()
    pltpu.make_async_copy(bulk, bulk, send_sem).wait()


def whole(space=pltpu.VMEM):
    return pl.BlockSpec(memory_space=space)


def all_to_all(value, number):
    shaped = value.reshape(SLABS, 16, LANES)
    result = pl.pallas_call(
        exchange,
        out_shape=jax.ShapeDtypeStruct(shaped.shape, F32),
        in_specs=[whole()],
        out_specs=whole(),
        scratch_shapes=[pltpu.SemaphoreType.DMA] * 3,
        compiler_params=pltpu.CompilerParams(
            collective_id=number, has_side_effects=True, vmem_limit_bytes=VMEM_BYTES
        ),
        name="all_to_all",
    )(shaped)
    return result.reshape(SLABS * 16, LANES)


def call(body, outs, scratch, *args, smem=()):
    return pl.pallas_call(
        body,
        out_shape=outs,
        in_specs=[whole(pltpu.SMEM if i in smem else pltpu.VMEM) for i in range(len(args))],
        out_specs=jax.tree.map(lambda _: whole(), outs),
        scratch_shapes=scratch,
        compiler_params=pltpu.CompilerParams(vmem_limit_bytes=VMEM_BYTES),
        name=body.__name__,
    )(*args)


MESSAGE = jax.ShapeDtypeStruct((SLABS * 16, LANES), F32)
FIELD = jax.ShapeDtypeStruct((ROWS, NZ), F32)
SPECTRUM = jax.ShapeDtypeStruct((2, ROWS, NX), BF16)
MIDDLE = pltpu.VMEM((2, 4, 256, LANES), F32)
WIDE = pltpu.VMEM((512, 256), F32)


def local(t, velocity, kernel, history, impedance, prestress, strength, fault_state):
    kernel, history = kernel[0], history[0]

    def first_kernel(field, z_first, forward_left, twiddle_rows, send):
        z_forward(field, send, dict(z_first=z_first, forward_left=forward_left, twiddle_rows=twiddle_rows))

    send = call(
        first_kernel, MESSAGE, [], velocity[0], t["z_first"], t["forward_left"], t["twiddle_rows"]
    )
    state = fault_state
    spec = None
    names = ("forward_right", "twiddle", "twiddle_rows", "x_second", "x_third", "inverse_left")
    for step in range(STEPS):
        received = all_to_all(send, 2 * step)
        if step == 0:

            def spectrum_first(received, kernel, history, a, b, c, d, e, f, send, spec, middle, wide):
                spectrum_phase(
                    0, received, kernel, history, spec, send, dict(zip(names, (a, b, c, d, e, f))), middle, wide
                )

            send, spec = call(
                spectrum_first,
                (MESSAGE, SPECTRUM),
                [MIDDLE, WIDE],
                received,
                kernel,
                history,
                *(t[n] for n in names),
            )
        else:

            def spectrum_second(received, kernel, history, spec, a, b, c, d, e, f, send, middle, wide):
                spectrum_phase(
                    1, received, kernel, history, spec, send, dict(zip(names, (a, b, c, d, e, f))), middle, wide
                )

            send = call(
                spectrum_second,
                MESSAGE,
                [MIDDLE, WIDE],
                received,
                kernel,
                history,
                spec,
                *(t[n] for n in names),
            )
        received = all_to_all(send, 2 * step + 1)

        def force_kernel(received, inverse_right, twiddle, z_last, force, middle):
            z_inverse(
                received, force, dict(inverse_right=inverse_right, twiddle=twiddle, z_last=z_last), middle
            )

        force = call(
            force_kernel, FIELD, [MIDDLE], received, t["inverse_right"], t["twiddle"], t["z_last"]
        )
        other = lax.ppermute(force, "side", [(0, 1), (1, 0)])

        def friction_kernel(
            impedance, force, other, prestress, strength, state, z_first, forward_left, twiddle_rows,
            speed, rate, state_out, send,
        ):
            friction(
                lax.axis_index("side") == 0, impedance, force, other, prestress, strength, state,
                speed, rate, state_out,
            )
            z_forward(speed, send, dict(z_first=z_first, forward_left=forward_left, twiddle_rows=twiddle_rows))

        def last_friction(impedance, force, other, prestress, strength, state, speed, rate, state_out):
            friction(
                lax.axis_index("side") == 0, impedance, force, other, prestress, strength, state,
                speed, rate, state_out,
            )

        fields = (impedance, force, other, prestress, strength, state)
        if step < STEPS - 1:
            speed, rate, state, send = call(
                friction_kernel, (FIELD, FIELD, FIELD, MESSAGE), [], *fields,
                t["z_first"], t["forward_left"], t["twiddle_rows"], smem=(0,),
            )
        else:
            speed, rate, state = call(last_friction, (FIELD, FIELD, FIELD), [], *fields, smem=(0,))
    return (speed[None], rate, state)


def solution(mesh):
    placed = (
        P("side", "slab", None),
        P("side", None, "slab", None),
        P("side", None, None, "slab", None),
        P(),
        P("slab", None),
        P("slab", None),
        P("slab", None),
    )
    constants = tables()

    def run(*args):
        return local({name: jnp.asarray(value) for name, value in constants.items()}, *args)

    return jax.shard_map(
        run,
        mesh=mesh,
        in_specs=placed,
        out_specs=(P("side", "slab", None), P("slab", None), P("slab", None)),
        check_vma=False,
    )
```

```python
import functools
import math

import jax
import jax.numpy as jnp
import ml_dtypes
import numpy as np
from jax import lax
from jax.experimental import pallas as pl
from jax.experimental.pallas import tpu as pltpu
from jax.sharding import PartitionSpec as P

NX = 4096
NZ = 4096
LAGS = 8
NEWTON = 4
STEPS = 2
SLABS = 128
ROWS = 32
LANES = 128
MESH = pl.DeviceIdType.MESH
F32 = jnp.float32
BF16 = jnp.bfloat16
VMEM_BYTES = 56 * 2**20


def high_low(table, axis):
    table = table.astype(np.float32)
    high = table.astype(ml_dtypes.bfloat16)
    low = (table - high.astype(np.float32)).astype(ml_dtypes.bfloat16)
    return np.concatenate([high, low, high], axis=axis)


def complex_matrix(count, sign):
    angle = 2.0 * math.pi / count * (np.outer(np.arange(count), np.arange(count)) % count)
    cos, sin = np.cos(angle), sign * np.sin(angle)
    return np.block([[cos, -sin], [sin, cos]])


def tables():
    forward, inverse = complex_matrix(128, -1.0), complex_matrix(128, 1.0)
    forward_32 = complex_matrix(32, -1.0).reshape(2, 32, 2, 32)
    inverse_32 = complex_matrix(32, 1.0).reshape(2, 32, 2, 32)
    eye = np.eye(8)
    z_first = np.einsum("ajn,xy->ajxny", forward_32[:, :, 0], eye).reshape(512, 256)
    x_second = np.einsum("akcgx,ij->akicgjx", forward_32.reshape(2, 32, 2, 4, 8), eye).reshape(512, 512)
    x_third = np.einsum("axck,ij->axickj", inverse_32, eye).reshape(512, 512)
    z_last = np.einsum("zcgj,xy->zxcgyj", inverse_32[0].reshape(32, 2, 4, 8), eye).reshape(256, 512) / (NX * NZ)
    phase = 2.0 * math.pi / 4096 * np.outer(np.arange(32), np.arange(128))
    twiddle = np.stack([np.cos(phase), np.sin(phase)]).astype(np.float32)
    return dict(
        z_first=high_low(z_first, 1),
        x_second=high_low(x_second, 1),
        x_third=high_low(x_third, 1),
        z_last=high_low(z_last, 1),
        forward_left=high_low(forward, 1),
        inverse_left=high_low(inverse, 1),
        forward_right=high_low(forward.T, 0),
        inverse_right=high_low(inverse.T, 0),
        twiddle=twiddle,
        twiddle_rows=np.repeat(twiddle, 8, axis=1),
    )


def split(value):
    high = value.astype(BF16)
    low = (value - high.astype(F32)).astype(BF16)
    return high, low


def left_product(table, value):
    high, low = split(value)
    stacked = jnp.concatenate([high, high, low], axis=0)
    return jnp.dot(table, stacked, preferred_element_type=F32)


def right_product(value, table):
    high, low = split(value)
    stacked = jnp.concatenate([high, high, low], axis=1)
    return jnp.dot(stacked, table, preferred_element_type=F32)


def left_product_transposed(table, value):
    high, low = split(value)
    stacked = jnp.concatenate([high, high, low], axis=1)
    return lax.dot_general(table, stacked, (((1,), (1,)), ((), ())), preferred_element_type=F32)


def turn(real, imag, cos, sin):
    return real * cos - imag * sin, real * sin + imag * cos


def put_group(chunks, fixed, value, by_half):
    for part in range(2):
        for half in range(2):
            chunk, rows = by_half(half)
            piece = value[part * 128 : part * 128 + 128, half * 128 : half * 128 + 128]
            chunks[chunk, pl.ds(rows * 4 + part * 2 + fixed, SLABS, stride=8), :] = piece


def get_pair(chunks, chunk, rows):
    return jnp.concatenate(
        [
            jnp.concatenate(
                [chunks[chunk, pl.ds(rows * 4 + part * 2 + q, SLABS, stride=8), :] for q in range(2)], axis=1
            )
            for part in range(2)
        ],
        axis=0,
    )


def z_forward(field, rows, send, t):
    cos, sin = t["twiddle_rows"][0], t["twiddle_rows"][1]
    columns = [
        jnp.concatenate(
            [field[group * 8 : group * 8 + 8, n * 128 : n * 128 + 128] for n in range(32)], axis=0
        )
        for group in (2 * rows, 2 * rows + 1)
    ]
    first = left_product(t["z_first"][...], jnp.concatenate(columns, axis=1))
    for q in range(2):
        piece = first[:, q * 128 : q * 128 + 128]
        real, imag = turn(piece[:256], piece[256:], cos, -sin)
        turned = jnp.concatenate([real, imag], axis=1)
        result = left_product_transposed(t["forward_left"][...], turned)
        put_group(send, q, result, lambda half: (half, rows))


def gather_stage(pieces, table, twiddle, sign, middle):
    for pair, piece in enumerate(pieces):
        first = right_product(piece().T, table[...])
        cos = twiddle[0, pair * 16 : pair * 16 + 16, :].reshape(2, 1, 8, 128)
        sin = sign * twiddle[1, pair * 16 : pair * 16 + 16, :].reshape(2, 1, 8, 128)
        real, imag = turn(
            first[:, :128].reshape(2, 16, 8, 128), first[:, 128:].reshape(2, 16, 8, 128), cos, sin
        )
        middle[0, 2 * pair : 2 * pair + 2] = real.reshape(2, 128, 128)
        middle[1, 2 * pair : 2 * pair + 2] = imag.reshape(2, 128, 128)


def middle_columns(middle):
    return jnp.concatenate(
        [
            jnp.concatenate(
                [middle[c, g, q * 64 : q * 64 + 64, :] for c in range(2) for g in range(4)], axis=0
            )
            for q in range(2)
        ],
        axis=1,
    )


def past_sums(kernel, history, sums):
    def add(k, carry):
        lanes = pl.ds(pl.multiple_of(k * 128, 128), 128)
        for pair in range(2):
            rows = slice(pair * 16, pair * 16 + 16)
            weights = [kernel[lag, rows, lanes].astype(F32) for lag in range(1, LAGS + 1)]
            for part in range(2):
                past = [history[lag, part, rows, lanes].astype(F32) for lag in range(LAGS)]
                first = weights[0] * past[0]
                for lag in range(1, LAGS):
                    first = first + weights[lag] * past[lag]
                second = weights[1] * past[0]
                for lag in range(2, LAGS):
                    second = second + weights[lag] * past[lag - 1]
                sums[0, part, rows, lanes] = first
                sums[1, part, rows, lanes] = second
        return carry

    lax.fori_loop(0, 32, add, 0)


def spectrum_phase(step, chunk, received, kernel, sums, send, t, middle, wide):
    gather_stage(
        [functools.partial(get_pair, received, chunk, rows) for rows in range(2)],
        t["forward_right"], t["twiddle"], -1.0, middle,
    )
    cos, sin = t["twiddle_rows"][0], t["twiddle_rows"][1]
    wide[...] = left_product(t["x_second"][...], middle_columns(middle))
    rows = slice(chunk * 16, chunk * 16 + 16)

    def convolve(k, carry):
        lanes = pl.ds(pl.multiple_of(k * 128, 128), 128)
        newest = kernel[0, rows, lanes].astype(F32)
        next_newest = kernel[1, rows, lanes].astype(F32)
        for part in range(2):
            place = pl.ds(pl.multiple_of(part * 256 + k * 8, 8), 8)
            fresh = wide[place, :]
            rounded = jnp.concatenate([fresh[:, :128], fresh[:, 128:]], axis=0).astype(BF16).astype(F32)
            total = newest * rounded + sums[step, part, rows, lanes]
            if step + 1 < STEPS:
                sums[step + 1, part, rows, lanes] = sums[step + 1, part, rows, lanes] + next_newest * rounded
            wide[place, :] = jnp.concatenate([total[:8], total[8:]], axis=1)
        return carry

    lax.fori_loop(0, 32, convolve, 0)
    third = left_product(t["x_third"][...], wide[...])
    for q in range(2):
        piece = third[:, q * 128 : q * 128 + 128]
        real, imag = turn(piece[:256], piece[256:], cos, sin)
        turned = jnp.concatenate([real, imag], axis=1)
        result = left_product_transposed(t["inverse_left"][...], turned)
        put_group(send, q, result, lambda half: (chunk, half))


def z_inverse(received, rows, force, t, middle):
    gather_stage(
        [functools.partial(get_pair, received, chunk, rows) for chunk in range(2)],
        t["inverse_right"], t["twiddle"], 1.0, middle,
    )
    last = left_product(t["z_last"][...], middle_columns(middle))
    for q in range(2):
        group = 2 * rows + q
        for n in range(32):
            force[group * 8 : group * 8 + 8, n * 128 : n * 128 + 128] = last[
                n * 8 : n * 8 + 8, q * 128 : q * 128 + 128
            ]


def friction(rows, is_first, impedance, force, other, prestress, strength, state, speed, rate_out):
    eta_first, eta_second = impedance[0], impedance[1]
    eta_total = eta_first + eta_second
    weight_first = eta_second / eta_total
    weight_second = eta_first / eta_total
    eta_joint = eta_first * eta_second / eta_total
    own_weight = jnp.where(is_first, weight_first, weight_second)
    other_weight = jnp.where(is_first, weight_second, weight_first)
    own_scale = jnp.where(is_first, 1.0 / eta_first, -1.0 / eta_second)

    def solve(index, carry):
        row = rows * 16 + pl.multiple_of(lax.rem(index, 2) * 8, 8)
        lane = pl.multiple_of(lax.div(index, 2) * 512, 512)
        at = (pl.ds(row, 8), pl.ds(lane, 512))
        own = force[at]
        stress_now = prestress[at]
        normal = strength[at]
        psi = state[at]
        locked = stress_now + (own_weight * own + other_weight * other[at])
        rate = locked / (eta_joint + normal)
        factor = 0.5 * jnp.exp(psi)
        normal_factor = normal * factor
        for _ in range(NEWTON):
            scaled = factor * rate
            magnitude = jnp.abs(scaled)
            square = magnitude * magnitude
            root = jnp.sqrt(1.0 + square)
            arc = jnp.log1p(magnitude + square / (1.0 + root))
            arc = jnp.where(scaled < 0.0, -arc, arc)
            misfit = normal * arc + eta_joint * rate - locked
            slope = normal_factor / root + eta_joint
            rate = rate - 0.5 * misfit / slope
        stress = locked - eta_joint * rate
        speed[at] = (stress_now + own - stress) * own_scale
        rate_out[at] = rate
        state[at] = psi + 0.25 * (jnp.exp(-psi) - jnp.abs(rate))
        return carry

    lax.fori_loop(0, 16, solve, 0)


TABLES = (
    "z_first", "forward_left", "twiddle_rows", "forward_right", "twiddle",
    "x_second", "x_third", "inverse_left", "inverse_right", "z_last",
)
FIELDS = ("velocity", "kernel", "history", "prestress", "strength", "state")


def simulate(*refs):
    count = len(TABLES) + len(FIELDS)
    impedance = refs[0]
    outside = refs[1 : 1 + count]
    speed_out, rate_out, state_out = refs[1 + count : 4 + count]
    inside = refs[4 + count : 4 + 2 * count]
    (send, recv, middle, wide, sums, force, other,
     load_sem, own_sem, send_sem, recv_sem, side_send_sem, side_recv_sem) = refs[4 + 2 * count :]
    names = FIELDS[:1] + TABLES[:3] + FIELDS[1:3] + TABLES[3:] + FIELDS[3:]
    t = dict(zip(names, inside))
    me = lax.axis_index("slab")
    side = lax.axis_index("side")
    barrier = pltpu.get_barrier_semaphore()

    def greet(i, carry):
        there = lax.rem(me + i, SLABS)
        pl.semaphore_signal(barrier, inc=1, device_id=(side, there), device_id_type=MESH)
        return carry

    pl.semaphore_signal(barrier, inc=1, device_id=(1 - side, me), device_id_type=MESH)
    lax.fori_loop(1, SLABS, greet, 0)

    loads = {
        name: pltpu.make_async_copy(outside[k], inside[k], load_sem.at[k]) for k, name in enumerate(names)
    }
    for name in names:
        loads[name].start()

    def need(*wanted):
        for name in wanted:
            loads.pop(name).wait()

    def start(stage, chunk):
        def one(i, carry):
            there = lax.rem(me + i, SLABS)
            pltpu.make_async_remote_copy(
                src_ref=send.at[stage, chunk, pl.ds(pl.multiple_of(there * 8, 8), 8)],
                dst_ref=recv.at[stage, chunk, pl.ds(pl.multiple_of(me * 8, 8), 8)],
                send_sem=send_sem.at[stage, chunk],
                recv_sem=recv_sem.at[stage, chunk],
                device_id=(side, there),
                device_id_type=MESH,
            ).start()
            return carry

        lax.fori_loop(1, SLABS, one, 0)
        own(stage, chunk).start()

    def own(stage, chunk):
        mine = pl.ds(pl.multiple_of(me * 8, 8), 8)
        return pltpu.make_async_copy(
            send.at[stage, chunk, mine], recv.at[stage, chunk, mine], own_sem.at[stage, chunk]
        )

    def arrived(stage, chunk):
        own(stage, chunk).wait()
        bulk = recv.at[stage, chunk, pl.ds(0, (SLABS - 1) * 8)]
        pltpu.make_async_copy(bulk, bulk, recv_sem.at[stage, chunk]).wait()

    def left(stage, chunk):
        bulk = send.at[stage, chunk, pl.ds(0, (SLABS - 1) * 8)]
        pltpu.make_async_copy(bulk, bulk, send_sem.at[stage, chunk]).wait()

    def across(step, rows):
        place = pl.ds(rows * 16, 16)
        return pltpu.make_async_remote_copy(
            src_ref=force.at[step, place],
            dst_ref=other.at[step, place],
            send_sem=side_send_sem.at[step, rows],
            recv_sem=side_recv_sem.at[step, rows],
            device_id=(1 - side, me),
            device_id_type=MESH,
        )

    need("velocity", "z_first", "forward_left", "twiddle_rows")
    for rows in range(2):
        z_forward(t["velocity"], rows, send.at[0], t)
    pl.semaphore_wait(barrier, SLABS)
    for chunk in range(2):
        start(0, chunk)
    need("kernel", "history")
    past_sums(t["kernel"], t["history"], sums)
    need(*tuple(loads))
    for step in range(STEPS):
        there, back = 2 * step, 2 * step + 1
        for chunk in range(2):
            arrived(there, chunk)
            spectrum_phase(step, chunk, recv.at[there], t["kernel"], sums, send.at[back], t, middle, wide)
            start(back, chunk)
        for chunk in range(2):
            arrived(back, chunk)
        for rows in range(2):
            z_inverse(recv.at[back], rows, force.at[step], t, middle)
            across(step, rows).start()
        for rows in range(2):
            across(step, rows).wait_recv()
            last = step == STEPS - 1
            friction(
                rows, side == 0, impedance, force.at[step], other.at[step], t["prestress"], t["strength"],
                t["state"], speed_out if last else t["velocity"], rate_out,
            )
            if not last:
                z_forward(t["velocity"], rows, send.at[2 * step + 2], t)
        if not last:
            for chunk in range(2):
                start(2 * step + 2, chunk)
    state_out[...] = t["state"][...]
    for stage in range(2 * STEPS):
        for chunk in range(2):
            left(stage, chunk)
    for step in range(STEPS):
        for rows in range(2):
            across(step, rows).wait_send()


def whole(space=pltpu.VMEM):
    return pl.BlockSpec(memory_space=space)


def local(t, velocity, kernel, history, impedance, prestress, strength, fault_state):
    given = dict(
        t,
        velocity=velocity[0], kernel=kernel[0], history=history[0],
        prestress=prestress, strength=strength, state=fault_state,
    )
    names = FIELDS[:1] + TABLES[:3] + FIELDS[1:3] + TABLES[3:] + FIELDS[3:]
    values = [given[name] for name in names]
    field = jax.ShapeDtypeStruct((ROWS, NZ), F32)
    semaphores = pltpu.SemaphoreType.DMA
    speed, rate, state = pl.pallas_call(
        simulate,
        out_shape=(field, field, field),
        in_specs=[whole(pltpu.SMEM)] + [whole(pl.ANY)] * len(values),
        out_specs=(whole(), whole(), whole()),
        scratch_shapes=[pltpu.VMEM(v.shape, v.dtype) for v in values]
        + [
            pltpu.VMEM((2 * STEPS, 2, SLABS * 8, LANES), F32),
            pltpu.VMEM((2 * STEPS, 2, SLABS * 8, LANES), F32),
            pltpu.VMEM((2, 4, 128, LANES), F32),
            pltpu.VMEM((512, 256), F32),
            pltpu.VMEM((STEPS, 2, ROWS, NX), F32),
            pltpu.VMEM((STEPS, ROWS, NZ), F32),
            pltpu.VMEM((STEPS, ROWS, NZ), F32),
            semaphores((len(values),)),
            semaphores((2 * STEPS, 2)),
            semaphores((2 * STEPS, 2)),
            semaphores((2 * STEPS, 2)),
            semaphores((STEPS, 2)),
            semaphores((STEPS, 2)),
        ],
        compiler_params=pltpu.CompilerParams(
            collective_id=0, has_side_effects=True, vmem_limit_bytes=VMEM_BYTES
        ),
        name="simulate",
    )(impedance, *values)
    return (speed[None], rate, state)


def solution(mesh):
    placed = (
        P("side", "slab", None),
        P("side", None, "slab", None),
        P("side", None, None, "slab", None),
        P(),
        P("slab", None),
        P("slab", None),
        P("slab", None),
    )
    constants = tables()

    def run(*args):
        return local({name: jnp.asarray(value) for name, value in constants.items()}, *args)

    return jax.shard_map(
        run,
        mesh=mesh,
        in_specs=placed,
        out_specs=(P("side", "slab", None), P("slab", None), P("slab", None)),
        check_vma=False,
    )
```

```python
import functools
import math

import jax
import jax.numpy as jnp
import ml_dtypes
import numpy as np
from jax import lax
from jax.experimental import pallas as pl
from jax.experimental.pallas import tpu as pltpu
from jax.sharding import PartitionSpec as P

NX = 4096
NZ = 4096
LAGS = 8
NEWTON = 4
STEPS = 2
SLABS = 128
ROWS = 32
LANES = 128
MESH = pl.DeviceIdType.MESH
F32 = jnp.float32
BF16 = jnp.bfloat16
VMEM_BYTES = 40 * 2**20


def high_low(table, axis):
    table = table.astype(np.float32)
    high = table.astype(ml_dtypes.bfloat16)
    low = (table - high.astype(np.float32)).astype(ml_dtypes.bfloat16)
    return np.concatenate([high, low, high], axis=axis)


def complex_matrix(count, sign):
    angle = 2.0 * math.pi / count * (np.outer(np.arange(count), np.arange(count)) % count)
    cos, sin = np.cos(angle), sign * np.sin(angle)
    return np.block([[cos, -sin], [sin, cos]])


def tables():
    forward, inverse = complex_matrix(128, -1.0), complex_matrix(128, 1.0)
    forward_32 = complex_matrix(32, -1.0).reshape(2, 32, 2, 32)
    inverse_32 = complex_matrix(32, 1.0).reshape(2, 32, 2, 32)
    eye = np.eye(8)
    z_first = np.einsum("ajn,xy->ajxny", forward_32[:, :, 0], eye).reshape(512, 256)
    x_second = np.einsum("akcgx,ij->akicgjx", forward_32.reshape(2, 32, 2, 4, 8), eye).reshape(512, 512)
    x_third = np.einsum("axck,ij->axickj", inverse_32, eye).reshape(512, 512)
    z_last = np.einsum("zcgj,xy->zxcgyj", inverse_32[0].reshape(32, 2, 4, 8), eye).reshape(256, 512) / (NX * NZ)
    phase = 2.0 * math.pi / 4096 * np.outer(np.arange(32), np.arange(128))
    twiddle = np.stack([np.cos(phase), np.sin(phase)]).astype(np.float32)
    return dict(
        z_first=high_low(z_first, 1),
        x_second=high_low(x_second, 1),
        x_third=high_low(x_third, 1),
        z_last=high_low(z_last, 1),
        forward_left=high_low(forward, 1),
        inverse_left=high_low(inverse, 1),
        forward_right=high_low(forward.T, 0),
        inverse_right=high_low(inverse.T, 0),
        twiddle=twiddle,
        twiddle_rows=np.repeat(twiddle, 8, axis=1),
    )


def split(value):
    high = value.astype(BF16)
    low = (value - high.astype(F32)).astype(BF16)
    return high, low


def left_product(table, value):
    high, low = split(value)
    stacked = jnp.concatenate([high, high, low], axis=0)
    return jnp.dot(table, stacked, preferred_element_type=F32)


def right_product(value, table):
    high, low = split(value)
    stacked = jnp.concatenate([high, high, low], axis=1)
    return jnp.dot(stacked, table, preferred_element_type=F32)


def left_product_transposed(table, value):
    high, low = split(value)
    stacked = jnp.concatenate([high, high, low], axis=1)
    return lax.dot_general(table, stacked, (((1,), (1,)), ((), ())), preferred_element_type=F32)


def turn(real, imag, cos, sin):
    return real * cos - imag * sin, real * sin + imag * cos


def flat(chunks, chunk):
    return chunks.at[chunk].reshape(SLABS * 8, LANES)


def put_group(chunks, fixed, value, by_half):
    for part in range(2):
        for half in range(2):
            chunk, rows = by_half(half)
            piece = value[part * 128 : part * 128 + 128, half * 128 : half * 128 + 128]
            flat(chunks, chunk)[pl.ds(rows * 4 + part * 2 + fixed, SLABS, stride=8), :] = piece


def get_pair(chunks, chunk, rows):
    ref = flat(chunks, chunk)
    return jnp.concatenate(
        [
            jnp.concatenate(
                [ref[pl.ds(rows * 4 + part * 2 + q, SLABS, stride=8), :] for q in range(2)], axis=1
            )
            for part in range(2)
        ],
        axis=0,
    )


def z_forward(field, rows, send, t):
    cos, sin = t["twiddle_rows"][0], t["twiddle_rows"][1]
    columns = [
        jnp.concatenate(
            [field[group * 8 : group * 8 + 8, n * 128 : n * 128 + 128] for n in range(32)], axis=0
        )
        for group in (2 * rows, 2 * rows + 1)
    ]
    first = left_product(t["z_first"][...], jnp.concatenate(columns, axis=1))
    for q in range(2):
        piece = first[:, q * 128 : q * 128 + 128]
        real, imag = turn(piece[:256], piece[256:], cos, -sin)
        turned = jnp.concatenate([real, imag], axis=1)
        result = left_product_transposed(t["forward_left"][...], turned)
        put_group(send, q, result, lambda half: (half, rows))


def gather_stage(pieces, table, twiddle, sign, middle):
    for pair, piece in enumerate(pieces):
        first = right_product(piece().T, table[...])
        cos = twiddle[0, pair * 16 : pair * 16 + 16, :].reshape(2, 1, 8, 128)
        sin = sign * twiddle[1, pair * 16 : pair * 16 + 16, :].reshape(2, 1, 8, 128)
        real, imag = turn(
            first[:, :128].reshape(2, 16, 8, 128), first[:, 128:].reshape(2, 16, 8, 128), cos, sin
        )
        middle[0, 2 * pair : 2 * pair + 2] = real.reshape(2, 128, 128)
        middle[1, 2 * pair : 2 * pair + 2] = imag.reshape(2, 128, 128)


def middle_columns(middle):
    return jnp.concatenate(
        [
            jnp.concatenate(
                [middle[c, g, q * 64 : q * 64 + 64, :] for c in range(2) for g in range(4)], axis=0
            )
            for q in range(2)
        ],
        axis=1,
    )


def past_sums(kernel, history, sums):
    def add(k, carry):
        lanes = pl.ds(pl.multiple_of(k * 128, 128), 128)
        for pair in range(2):
            rows = slice(pair * 16, pair * 16 + 16)
            weights = [kernel[lag, rows, lanes].astype(F32) for lag in range(1, LAGS + 1)]
            for part in range(2):
                past = [history[lag, part, rows, lanes].astype(F32) for lag in range(LAGS)]
                first = weights[0] * past[0]
                for lag in range(1, LAGS):
                    first = first + weights[lag] * past[lag]
                second = weights[1] * past[0]
                for lag in range(2, LAGS):
                    second = second + weights[lag] * past[lag - 1]
                sums[0, part, rows, lanes] = first
                sums[1, part, rows, lanes] = second
        return carry

    lax.fori_loop(0, 32, add, 0)


def spectrum_phase(step, chunk, received, kernel, sums, send, t, middle, wide):
    gather_stage(
        [functools.partial(get_pair, received, chunk, rows) for rows in range(2)],
        t["forward_right"], t["twiddle"], -1.0, middle,
    )
    cos, sin = t["twiddle_rows"][0], t["twiddle_rows"][1]
    wide[...] = left_product(t["x_second"][...], middle_columns(middle))
    rows = slice(chunk * 16, chunk * 16 + 16)

    def convolve(k, carry):
        lanes = pl.ds(pl.multiple_of(k * 128, 128), 128)
        newest = kernel[0, rows, lanes].astype(F32)
        next_newest = kernel[1, rows, lanes].astype(F32)
        for part in range(2):
            place = pl.ds(pl.multiple_of(part * 256 + k * 8, 8), 8)
            fresh = wide[place, :]
            rounded = jnp.concatenate([fresh[:, :128], fresh[:, 128:]], axis=0).astype(BF16).astype(F32)
            total = newest * rounded + sums[step, part, rows, lanes]
            if step + 1 < STEPS:
                sums[step + 1, part, rows, lanes] = sums[step + 1, part, rows, lanes] + next_newest * rounded
            wide[place, :] = jnp.concatenate([total[:8], total[8:]], axis=1)
        return carry

    lax.fori_loop(0, 32, convolve, 0, unroll=2)
    third = left_product(t["x_third"][...], wide[...])
    for q in range(2):
        piece = third[:, q * 128 : q * 128 + 128]
        real, imag = turn(piece[:256], piece[256:], cos, sin)
        turned = jnp.concatenate([real, imag], axis=1)
        result = left_product_transposed(t["inverse_left"][...], turned)
        put_group(send, q, result, lambda half: (chunk, half))


def z_inverse(received, rows, force, t, middle):
    gather_stage(
        [functools.partial(get_pair, received, chunk, rows) for chunk in range(2)],
        t["inverse_right"], t["twiddle"], 1.0, middle,
    )
    last = left_product(t["z_last"][...], middle_columns(middle))
    for q in range(2):
        group = 2 * rows + q
        for n in range(32):
            force[group * 8 : group * 8 + 8, n * 128 : n * 128 + 128] = last[
                n * 8 : n * 8 + 8, q * 128 : q * 128 + 128
            ]


def friction(rows, is_first, impedance, force, other, prestress, strength, state, speed, rate_out):
    eta_first, eta_second = impedance[0], impedance[1]
    eta_total = eta_first + eta_second
    weight_first = eta_second / eta_total
    weight_second = eta_first / eta_total
    eta_joint = eta_first * eta_second / eta_total
    own_weight = jnp.where(is_first, weight_first, weight_second)
    other_weight = jnp.where(is_first, weight_second, weight_first)
    own_scale = jnp.where(is_first, 1.0 / eta_first, -1.0 / eta_second)

    def solve(index, carry):
        row = rows * 16 + pl.multiple_of(lax.rem(index, 2) * 8, 8)
        lane = pl.multiple_of(lax.div(index, 2) * 512, 512)
        at = (pl.ds(row, 8), pl.ds(lane, 512))
        own = force[at]
        stress_now = prestress[at]
        normal = strength[at]
        psi = state[at]
        locked = stress_now + (own_weight * own + other_weight * other[at])
        rate = locked / (eta_joint + normal)
        factor = 0.5 * jnp.exp(psi)
        normal_factor = normal * factor
        for _ in range(NEWTON):
            scaled = factor * rate
            root = jnp.sqrt(1.0 + scaled * scaled)
            arc = jnp.log(jnp.abs(scaled) + root)
            arc = jnp.where(scaled < 0.0, -arc, arc)
            misfit = normal * arc + eta_joint * rate - locked
            rate = rate - 0.5 * misfit * root / (normal_factor + eta_joint * root)
        stress = locked - eta_joint * rate
        speed[at] = (stress_now + own - stress) * own_scale
        rate_out[at] = rate
        state[at] = psi + 0.25 * (jnp.exp(-psi) - jnp.abs(rate))
        return carry

    lax.fori_loop(0, 16, solve, 0)


TABLES = (
    "z_first", "forward_left", "twiddle_rows", "forward_right", "twiddle",
    "x_second", "x_third", "inverse_left", "inverse_right", "z_last",
)
FIELDS = ("velocity", "kernel", "history", "prestress", "strength", "state")


def simulate(*refs):
    count = len(TABLES) + len(FIELDS)
    impedance = refs[0]
    outside = refs[1 : 1 + count]
    speed_out, rate_out, state_out = refs[1 + count : 4 + count]
    inside = refs[4 + count : 4 + 2 * count]
    (send, recv, middle, wide, sums, force, other,
     load_sem, own_sem, send_sem, recv_sem, side_send_sem, side_recv_sem) = refs[4 + 2 * count :]
    names = FIELDS[:1] + TABLES[:3] + FIELDS[1:3] + TABLES[3:] + FIELDS[3:]
    t = dict(zip(names, inside))
    me = lax.axis_index("slab")
    side = lax.axis_index("side")
    barrier = pltpu.get_barrier_semaphore()

    def greet(i, carry):
        there = lax.rem(me + i, SLABS)
        pl.semaphore_signal(barrier, inc=1, device_id=(side, there), device_id_type=MESH)
        return carry

    loads = {
        name: pltpu.make_async_copy(outside[k], inside[k], load_sem.at[k]) for k, name in enumerate(names)
    }
    for name in names[:4]:
        loads[name].start()
    pl.semaphore_signal(barrier, inc=1, device_id=(1 - side, me), device_id_type=MESH)
    lax.fori_loop(1, SLABS, greet, 0, unroll=4)

    def need(*wanted):
        for name in wanted:
            loads.pop(name).wait()

    def place(name, where):
        return {
            "first rows": (slice(None), where, pl.ds(0, 4)),
            "first waves": (0, where),
            "mixed": (0, where, pl.ds(4, 4)) if name[0] == "out" else (1, where, pl.ds(0, 4)),
            "last": (1, where, pl.ds(4, 4)),
        }[name[1]]

    def own(stage, name, index):
        mine = place(name, me)
        return pltpu.make_async_copy(
            send.at[(stage,) + mine], recv.at[(stage,) + mine], own_sem.at[stage, index]
        )

    def start(stage, name, index):
        def one(i, carry):
            there = lax.rem(me + i, SLABS)
            pltpu.make_async_remote_copy(
                src_ref=send.at[(stage,) + place(name, there)],
                dst_ref=recv.at[(stage,) + place(name, me)],
                send_sem=send_sem.at[stage, index],
                recv_sem=recv_sem.at[stage, index],
                device_id=(side, there),
                device_id_type=MESH,
            ).start()
            return carry

        lax.fori_loop(1, SLABS, one, 0, unroll=4)
        own(stage, name, index).start()

    def arrived(stage, name, index):
        own(stage, name, index).wait()
        bulk = recv.at[(stage,) + place(name, pl.ds(0, SLABS - 1))]
        pltpu.make_async_copy(bulk, bulk, recv_sem.at[stage, index]).wait()

    def left(stage, name, index):
        bulk = send.at[(stage,) + place(name, pl.ds(0, SLABS - 1))]
        pltpu.make_async_copy(bulk, bulk, send_sem.at[stage, index]).wait()

    out_names = [("out", "first rows"), ("out", "mixed"), ("out", "last")]
    back_names = [("back", "first waves"), ("back", "mixed"), ("back", "last")]

    def across(step, rows):
        place = pl.ds(rows * 16, 16)
        return pltpu.make_async_remote_copy(
            src_ref=force.at[step, place],
            dst_ref=other.at[step, place],
            send_sem=side_send_sem.at[step, rows],
            recv_sem=side_recv_sem.at[step, rows],
            device_id=(1 - side, me),
            device_id_type=MESH,
        )

    def send_rows(stage, rows):
        if rows == 0:
            start(stage, out_names[0], 0)
        else:
            start(stage, out_names[1], 1)
            start(stage, out_names[2], 2)

    need(*names[:4])
    for name in names[4:]:
        loads[name].start()
    z_forward(t["velocity"], 0, send.at[0], t)
    pl.semaphore_wait(barrier, SLABS)
    send_rows(0, 0)
    z_forward(t["velocity"], 1, send.at[0], t)
    send_rows(0, 1)
    need("kernel", "history")
    past_sums(t["kernel"], t["history"], sums)
    need(*tuple(loads))
    for step in range(STEPS):
        there, back = 2 * step, 2 * step + 1
        last = step == STEPS - 1
        arrived(there, out_names[0], 0)
        arrived(there, out_names[1], 1)
        spectrum_phase(step, 0, recv.at[there], t["kernel"], sums, send.at[back], t, middle, wide)
        start(back, back_names[0], 0)
        arrived(there, out_names[2], 2)
        spectrum_phase(step, 1, recv.at[there], t["kernel"], sums, send.at[back], t, middle, wide)
        start(back, back_names[1], 1)
        start(back, back_names[2], 2)
        arrived(back, back_names[0], 0)
        for rows in range(2):
            arrived(back, back_names[1 + rows], 1 + rows)
            z_inverse(recv.at[back], rows, force.at[step], t, middle)
            across(step, rows).start()
        for rows in range(2):
            across(step, rows).wait_recv()
            friction(
                rows, side == 0, impedance, force.at[step], other.at[step], t["prestress"], t["strength"],
                t["state"], speed_out if last else t["velocity"], rate_out,
            )
            if not last:
                z_forward(t["velocity"], rows, send.at[2 * step + 2], t)
                send_rows(2 * step + 2, rows)
    state_out[...] = t["state"][...]
    for stage in range(2 * STEPS):
        for index, name in enumerate(back_names if stage % 2 else out_names):
            left(stage, name, index)
    for step in range(STEPS):
        for rows in range(2):
            across(step, rows).wait_send()


def hand_over(*refs):
    for source, target in zip(refs[:3], refs[3:]):
        target[...] = source[...]


def whole(space=pltpu.VMEM):
    return pl.BlockSpec(memory_space=space)


def local(t, velocity, kernel, history, impedance, prestress, strength, fault_state):
    given = dict(
        t,
        velocity=velocity[0], kernel=kernel[0], history=history[0],
        prestress=prestress, strength=strength, state=fault_state,
    )
    names = FIELDS[:1] + TABLES[:3] + FIELDS[1:3] + TABLES[3:] + FIELDS[3:]
    values = [given[name] for name in names]
    field = jax.ShapeDtypeStruct((ROWS, NZ), F32)
    semaphores = pltpu.SemaphoreType.DMA
    results = pl.pallas_call(
        simulate,
        out_shape=(field, field, field),
        in_specs=[whole(pltpu.SMEM)] + [whole(pl.ANY)] * len(values),
        out_specs=(whole(), whole(), whole()),
        scratch_shapes=[pltpu.VMEM(v.shape, v.dtype) for v in values]
        + [
            pltpu.VMEM((2 * STEPS, 2, SLABS, 8, LANES), F32),
            pltpu.VMEM((2 * STEPS, 2, SLABS, 8, LANES), F32),
            pltpu.VMEM((2, 4, 128, LANES), F32),
            pltpu.VMEM((512, 256), F32),
            pltpu.VMEM((STEPS, 2, ROWS, NX), F32),
            pltpu.VMEM((STEPS, ROWS, NZ), F32),
            pltpu.VMEM((STEPS, ROWS, NZ), F32),
            semaphores((len(values),)),
            semaphores((2 * STEPS, 3)),
            semaphores((2 * STEPS, 3)),
            semaphores((2 * STEPS, 3)),
            semaphores((STEPS, 2)),
            semaphores((STEPS, 2)),
        ],
        compiler_params=pltpu.CompilerParams(
            collective_id=0, has_side_effects=True, vmem_limit_bytes=VMEM_BYTES
        ),
        name="simulate",
    )(impedance, *values)
    speed, rate, state = pl.pallas_call(
        hand_over,
        out_shape=(field, field, field),
        in_specs=[whole()] * 3,
        out_specs=(whole(),) * 3,
        compiler_params=pltpu.CompilerParams(vmem_limit_bytes=8 * 2**20),
        name="hand_over",
    )(*results)
    return (speed[None], rate, state)


def solution(mesh):
    placed = (
        P("side", "slab", None),
        P("side", None, "slab", None),
        P("side", None, None, "slab", None),
        P(),
        P("slab", None),
        P("slab", None),
        P("slab", None),
    )
    constants = tables()

    def run(*args):
        return local({name: jnp.asarray(value) for name, value in constants.items()}, *args)

    return jax.shard_map(
        run,
        mesh=mesh,
        in_specs=placed,
        out_specs=(P("side", "slab", None), P("slab", None), P("slab", None)),
        check_vma=False,
    )
```

```python
import functools
import math

import jax
import jax.numpy as jnp
import ml_dtypes
import numpy as np
from jax import lax
from jax.experimental import pallas as pl
from jax.experimental.pallas import tpu as pltpu
from jax.sharding import PartitionSpec as P

NX = 4096
NZ = 4096
LAGS = 8
NEWTON = 4
STEPS = 2
SLABS = 128
ROWS = 32
LANES = 128
MESH = pl.DeviceIdType.MESH
F32 = jnp.float32
BF16 = jnp.bfloat16
VMEM_BYTES = 56 * 2**20


def high_low(table, axis):
    table = table.astype(np.float32)
    high = table.astype(ml_dtypes.bfloat16)
    low = (table - high.astype(np.float32)).astype(ml_dtypes.bfloat16)
    return np.concatenate([high, low, high], axis=axis)


def complex_matrix(count, sign):
    angle = 2.0 * math.pi / count * (np.outer(np.arange(count), np.arange(count)) % count)
    cos, sin = np.cos(angle), sign * np.sin(angle)
    return np.block([[cos, -sin], [sin, cos]])


def tables():
    forward, inverse = complex_matrix(128, -1.0), complex_matrix(128, 1.0)
    forward_32 = complex_matrix(32, -1.0).reshape(2, 32, 2, 32)
    inverse_32 = complex_matrix(32, 1.0).reshape(2, 32, 2, 32)
    eye = np.eye(8)
    z_first = np.einsum("ajn,xy->ajxny", forward_32[:, :, 0], eye).reshape(512, 256)
    x_second = np.einsum("akcgx,ij->akicgjx", forward_32.reshape(2, 32, 2, 4, 8), eye).reshape(512, 512)
    x_third = np.einsum("axck,ij->axickj", inverse_32, eye).reshape(512, 512)
    z_last = np.einsum("zcgj,xy->zxcgyj", inverse_32[0].reshape(32, 2, 4, 8), eye).reshape(256, 512) / (NX * NZ)
    phase = 2.0 * math.pi / 4096 * np.outer(np.arange(32), np.arange(128))
    twiddle = np.stack([np.cos(phase), np.sin(phase)]).astype(np.float32)
    return dict(
        z_first=high_low(z_first, 1),
        x_second=high_low(x_second, 1),
        x_third=high_low(x_third, 1),
        z_last=high_low(z_last, 1),
        forward_left=high_low(forward, 1),
        inverse_left=high_low(inverse, 1),
        forward_right=high_low(forward.T, 0),
        inverse_right=high_low(inverse.T, 0),
        twiddle=twiddle,
        twiddle_rows=np.repeat(twiddle, 8, axis=1),
    )


def split(value):
    high = value.astype(BF16)
    low = (value - high.astype(F32)).astype(BF16)
    return high, low


def left_product(table, value):
    high, low = split(value)
    stacked = jnp.concatenate([high, high, low], axis=0)
    return jnp.dot(table, stacked, preferred_element_type=F32)


def right_product(value, table):
    high, low = split(value)
    stacked = jnp.concatenate([high, high, low], axis=1)
    return jnp.dot(stacked, table, preferred_element_type=F32)


def left_product_transposed(table, value):
    high, low = split(value)
    stacked = jnp.concatenate([high, high, low], axis=1)
    return lax.dot_general(table, stacked, (((1,), (1,)), ((), ())), preferred_element_type=F32)


def turn(real, imag, cos, sin):
    return real * cos - imag * sin, real * sin + imag * cos


def flat(chunks, chunk):
    return chunks.at[chunk].reshape(SLABS * 8, LANES)


def turned_rows(real, imag):
    return jnp.concatenate([real, imag], axis=1)


def z_forward(field, group, send, t):
    cos, sin = t["twiddle_rows"][0], t["twiddle_rows"][1]
    rows = slice(group * 8, group * 8 + 8)
    column = jnp.concatenate([field[rows, n * 128 : n * 128 + 128] for n in range(32)], axis=0)
    first = left_product(t["z_first"][...], column)
    real, imag = turn(first[:256], first[256:], cos, -sin)
    result = left_product_transposed(t["forward_left"][...], turned_rows(real, imag))
    for part in range(2):
        for chunk in range(2):
            flat(send, chunk)[pl.ds(group * 2 + part, SLABS, stride=8), :] = result[
                part * 128 : part * 128 + 128, chunk * 128 : chunk * 128 + 128
            ]


def fetch(chunks, places):
    return jnp.concatenate(
        [
            jnp.concatenate(
                [flat(chunks, chunk)[pl.ds(group * 2 + part, SLABS, stride=8), :] for chunk, group in places],
                axis=1,
            )
            for part in range(2)
        ],
        axis=0,
    )


def x_stage(received, chunk, t, middle):
    for pair in range(2):
        rows = fetch(received, [(chunk, 2 * pair), (chunk, 2 * pair + 1)]).T
        first = right_product(rows, t["forward_right"][...])
        cos = t["twiddle"][0, pair * 16 : pair * 16 + 16, :].reshape(2, 1, 8, 128)
        sin = t["twiddle"][1, pair * 16 : pair * 16 + 16, :].reshape(2, 1, 8, 128)
        real, imag = turn(
            first[:, :128].reshape(2, 16, 8, 128), first[:, 128:].reshape(2, 16, 8, 128), cos, -sin
        )
        middle[0, 2 * pair : 2 * pair + 2] = real.reshape(2, 128, 128)
        middle[1, 2 * pair : 2 * pair + 2] = imag.reshape(2, 128, 128)


def middle_columns(middle):
    return jnp.concatenate(
        [
            jnp.concatenate(
                [middle[c, g, q * 64 : q * 64 + 64, :] for c in range(2) for g in range(4)], axis=0
            )
            for q in range(2)
        ],
        axis=1,
    )


def past_sums(kernel, history, sums):
    def add(k, carry):
        lanes = pl.ds(pl.multiple_of(k * 128, 128), 128)
        for pair in range(2):
            rows = slice(pair * 16, pair * 16 + 16)
            weights = [kernel[lag, rows, lanes].astype(F32) for lag in range(1, LAGS + 1)]
            for part in range(2):
                past = [history[lag, part, rows, lanes].astype(F32) for lag in range(LAGS)]
                first = weights[0] * past[0]
                for lag in range(1, LAGS):
                    first = first + weights[lag] * past[lag]
                second = weights[1] * past[0]
                for lag in range(2, LAGS):
                    second = second + weights[lag] * past[lag - 1]
                sums[0, part, rows, lanes] = first
                sums[1, part, rows, lanes] = second
        return carry

    lax.fori_loop(0, 32, add, 0)


def spectrum_phase(step, chunk, received, kernel, sums, send, t, middle, wide):
    x_stage(received, chunk, t, middle)
    cos, sin = t["twiddle_rows"][0], t["twiddle_rows"][1]
    wide[...] = left_product(t["x_second"][...], middle_columns(middle))
    rows = slice(chunk * 16, chunk * 16 + 16)

    def convolve(k, carry):
        lanes = pl.ds(pl.multiple_of(k * 128, 128), 128)
        newest = kernel[0, rows, lanes].astype(F32)
        next_newest = kernel[1, rows, lanes].astype(F32)
        for part in range(2):
            place = pl.ds(pl.multiple_of(part * 256 + k * 8, 8), 8)
            fresh = wide[place, :]
            rounded = jnp.concatenate([fresh[:, :128], fresh[:, 128:]], axis=0).astype(BF16).astype(F32)
            total = newest * rounded + sums[step, part, rows, lanes]
            if step + 1 < STEPS:
                sums[step + 1, part, rows, lanes] = sums[step + 1, part, rows, lanes] + next_newest * rounded
            wide[place, :] = jnp.concatenate([total[:8], total[8:]], axis=1)
        return carry

    lax.fori_loop(0, 32, convolve, 0, unroll=2)
    third = left_product(t["x_third"][...], wide[...])
    turned = []
    for q in range(2):
        piece = third[:, q * 128 : q * 128 + 128]
        turned.append(turned_rows(*turn(piece[:256], piece[256:], cos, sin)))
    for pair in range(2):
        places = [slice((2 * pair + g) * 64, (2 * pair + g) * 64 + 64) for g in range(2)]
        ordered = jnp.concatenate([turned[q][place] for place in places for q in range(2)], axis=0)
        result = left_product_transposed(t["inverse_left"][...], ordered)
        for part in range(2):
            for g in range(2):
                flat(send, chunk)[pl.ds((2 * pair + g) * 2 + part, SLABS, stride=8), :] = result[
                    part * 128 : part * 128 + 128, g * 128 : g * 128 + 128
                ]


def z_inverse(received, group, force, t):
    rows = fetch(received, [(0, group), (1, group)]).T
    first = right_product(rows, t["inverse_right"][...])
    cos = t["twiddle"][0].reshape(4, 1, 8, 128)
    sin = t["twiddle"][1].reshape(4, 1, 8, 128)
    real, imag = turn(first[:, :128].reshape(4, 8, 8, 128), first[:, 128:].reshape(4, 8, 8, 128), cos, sin)
    column = jnp.concatenate([real.reshape(256, 128), imag.reshape(256, 128)], axis=0)
    last = left_product(t["z_last"][...], column)
    for n in range(32):
        force[group * 8 : group * 8 + 8, n * 128 : n * 128 + 128] = last[n * 8 : n * 8 + 8]


def friction(group, is_first, impedance, force, other, prestress, strength, state, speed, rate_out):
    eta_first, eta_second = impedance[0], impedance[1]
    eta_total = eta_first + eta_second
    weight_first = eta_second / eta_total
    weight_second = eta_first / eta_total
    eta_joint = eta_first * eta_second / eta_total
    own_weight = jnp.where(is_first, weight_first, weight_second)
    other_weight = jnp.where(is_first, weight_second, weight_first)
    own_scale = jnp.where(is_first, 1.0 / eta_first, -1.0 / eta_second)

    def solve(index, carry):
        at = (slice(group * 8, group * 8 + 8), pl.ds(pl.multiple_of(index * 512, 512), 512))
        own = force[at]
        stress_now = prestress[at]
        normal = strength[at]
        psi = state[at]
        locked = stress_now + (own_weight * own + other_weight * other[at])
        rate = locked / (eta_joint + normal)
        factor = 0.5 * jnp.exp(psi)
        normal_factor = normal * factor
        for _ in range(NEWTON):
            scaled = factor * rate
            root = jnp.sqrt(1.0 + scaled * scaled)
            arc = jnp.log(jnp.abs(scaled) + root)
            arc = jnp.where(scaled < 0.0, -arc, arc)
            misfit = normal * arc + eta_joint * rate - locked
            rate = rate - 0.5 * misfit * root / (normal_factor + eta_joint * root)
        stress = locked - eta_joint * rate
        speed[at] = (stress_now + own - stress) * own_scale
        rate_out[at] = rate
        state[at] = psi + 0.25 * (jnp.exp(-psi) - jnp.abs(rate))
        return carry

    lax.fori_loop(0, 8, solve, 0)


TABLES = (
    "z_first", "forward_left", "twiddle_rows", "forward_right", "twiddle",
    "x_second", "x_third", "inverse_left", "inverse_right", "z_last",
)
FIELDS = ("velocity", "kernel", "history", "prestress", "strength", "state")


def simulate(*refs):
    count = len(TABLES) + len(FIELDS)
    impedance = refs[0]
    outside = refs[1 : 1 + count]
    speed_out, rate_out, state_out = refs[1 + count : 4 + count]
    inside = refs[4 + count : 4 + 2 * count]
    (send, recv, middle, wide, sums, force, other,
     load_sem, own_sem, send_sem, recv_sem, side_send_sem, side_recv_sem) = refs[4 + 2 * count :]
    names = FIELDS[:1] + TABLES[:3] + FIELDS[1:3] + TABLES[3:] + FIELDS[3:]
    t = dict(zip(names, inside))
    me = lax.axis_index("slab")
    side = lax.axis_index("side")
    barrier = pltpu.get_barrier_semaphore()

    def greet(i, carry):
        there = lax.rem(me + i, SLABS)
        pl.semaphore_signal(barrier, inc=1, device_id=(side, there), device_id_type=MESH)
        return carry

    loads = {
        name: pltpu.make_async_copy(outside[k], inside[k], load_sem.at[k]) for k, name in enumerate(names)
    }
    for name in names[:4]:
        loads[name].start()
    pl.semaphore_signal(barrier, inc=1, device_id=(1 - side, me), device_id_type=MESH)
    lax.fori_loop(1, SLABS, greet, 0, unroll=4)

    def need(*wanted):
        for name in wanted:
            loads.pop(name).wait()

    def place(name, where):
        chunk, first, count = name
        return (chunk, where) if count == 4 else (chunk, where, pl.ds(first * 2, count * 2))

    def own(stage, name, index):
        mine = place(name, me)
        return pltpu.make_async_copy(
            send.at[(stage,) + mine], recv.at[(stage,) + mine], own_sem.at[stage, index]
        )

    def start(stage, name, index):
        def one(i, carry):
            there = lax.rem(me + i, SLABS)
            pltpu.make_async_remote_copy(
                src_ref=send.at[(stage,) + place(name, there)],
                dst_ref=recv.at[(stage,) + place(name, me)],
                send_sem=send_sem.at[stage, index],
                recv_sem=recv_sem.at[stage, index],
                device_id=(side, there),
                device_id_type=MESH,
            ).start()
            return carry

        lax.fori_loop(1, SLABS, one, 0, unroll=4)
        own(stage, name, index).start()

    def arrived(stage, name, index):
        own(stage, name, index).wait()
        bulk = recv.at[(stage,) + place(name, pl.ds(0, SLABS - 1))]
        pltpu.make_async_copy(bulk, bulk, recv_sem.at[stage, index]).wait()

    def left(stage, name, index):
        bulk = send.at[(stage,) + place(name, pl.ds(0, SLABS - 1))]
        pltpu.make_async_copy(bulk, bulk, send_sem.at[stage, index]).wait()

    both = slice(None)
    out_names = [(both, 0, 1), (both, 1, 1), (0, 2, 1), (0, 3, 1), (1, 2, 2)]
    back_names = [(0, 0, 4), (1, 0, 1), (1, 1, 1), (1, 2, 1), (1, 3, 1)]

    def across(step, rows):
        lines = pl.ds(rows * 8, 8)
        return pltpu.make_async_remote_copy(
            src_ref=force.at[step, lines],
            dst_ref=other.at[step, lines],
            send_sem=side_send_sem.at[step, rows],
            recv_sem=side_recv_sem.at[step, rows],
            device_id=(1 - side, me),
            device_id_type=MESH,
        )

    def send_rows(stage, group):
        start(stage, out_names[group], group)
        if group == 3:
            start(stage, out_names[4], 4)

    need(*names[:4])
    for name in names[4:]:
        loads[name].start()
    for group in range(4):
        z_forward(t["velocity"], group, send.at[0], t)
        if group == 0:
            pl.semaphore_wait(barrier, SLABS)
        send_rows(0, group)
    need("kernel", "history")
    past_sums(t["kernel"], t["history"], sums)
    need(*tuple(loads))
    for step in range(STEPS):
        there, back = 2 * step, 2 * step + 1
        last = step == STEPS - 1
        for index in range(4):
            arrived(there, out_names[index], index)
        spectrum_phase(step, 0, recv.at[there], t["kernel"], sums, send.at[back], t, middle, wide)
        start(back, back_names[0], 0)
        arrived(there, out_names[4], 4)
        spectrum_phase(step, 1, recv.at[there], t["kernel"], sums, send.at[back], t, middle, wide)
        for group in range(4):
            start(back, back_names[1 + group], 1 + group)
        arrived(back, back_names[0], 0)
        for group in range(4):
            arrived(back, back_names[1 + group], 1 + group)
            z_inverse(recv.at[back], group, force.at[step], t)
            across(step, group).start()
        for group in range(4):
            across(step, group).wait_recv()
            friction(
                group, side == 0, impedance, force.at[step], other.at[step], t["prestress"], t["strength"],
                t["state"], speed_out if last else t["velocity"], rate_out,
            )
            if not last:
                z_forward(t["velocity"], group, send.at[2 * step + 2], t)
                send_rows(2 * step + 2, group)
    state_out[...] = t["state"][...]
    for stage in range(2 * STEPS):
        for index, name in enumerate(back_names if stage % 2 else out_names):
            left(stage, name, index)
    for step in range(STEPS):
        for group in range(4):
            across(step, group).wait_send()


def hand_over(*refs):
    for source, target in zip(refs[:3], refs[3:]):
        target[...] = source[...]


def whole(space=pltpu.VMEM):
    return pl.BlockSpec(memory_space=space)


def local(t, velocity, kernel, history, impedance, prestress, strength, fault_state):
    given = dict(
        t,
        velocity=velocity[0], kernel=kernel[0], history=history[0],
        prestress=prestress, strength=strength, state=fault_state,
    )
    names = FIELDS[:1] + TABLES[:3] + FIELDS[1:3] + TABLES[3:] + FIELDS[3:]
    values = [given[name] for name in names]
    field = jax.ShapeDtypeStruct((ROWS, NZ), F32)
    semaphores = pltpu.SemaphoreType.DMA
    results = pl.pallas_call(
        simulate,
        out_shape=(field, field, field),
        in_specs=[whole(pltpu.SMEM)] + [whole(pl.ANY)] * len(values),
        out_specs=(whole(), whole(), whole()),
        scratch_shapes=[pltpu.VMEM(v.shape, v.dtype) for v in values]
        + [
            pltpu.VMEM((2 * STEPS, 2, SLABS, 8, LANES), F32),
            pltpu.VMEM((2 * STEPS, 2, SLABS, 8, LANES), F32),
            pltpu.VMEM((2, 4, 128, LANES), F32),
            pltpu.VMEM((512, 256), F32),
            pltpu.VMEM((STEPS, 2, ROWS, NX), F32),
            pltpu.VMEM((STEPS, ROWS, NZ), F32),
            pltpu.VMEM((STEPS, ROWS, NZ), F32),
            semaphores((len(values),)),
            semaphores((2 * STEPS, 5)),
            semaphores((2 * STEPS, 5)),
            semaphores((2 * STEPS, 5)),
            semaphores((STEPS, 4)),
            semaphores((STEPS, 4)),
        ],
        compiler_params=pltpu.CompilerParams(
            collective_id=0, has_side_effects=True, vmem_limit_bytes=VMEM_BYTES
        ),
        name="simulate",
    )(impedance, *values)
    speed, rate, state = pl.pallas_call(
        hand_over,
        out_shape=(field, field, field),
        in_specs=[whole()] * 3,
        out_specs=(whole(),) * 3,
        compiler_params=pltpu.CompilerParams(vmem_limit_bytes=VMEM_BYTES),
        name="hand_over",
    )(*results)
    return (speed[None], rate, state)


def solution(mesh):
    placed = (
        P("side", "slab", None),
        P("side", None, "slab", None),
        P("side", None, None, "slab", None),
        P(),
        P("slab", None),
        P("slab", None),
        P("slab", None),
    )
    constants = tables()

    def run(*args):
        return local({name: jnp.asarray(value) for name, value in constants.items()}, *args)

    return jax.shard_map(
        run,
        mesh=mesh,
        in_specs=placed,
        out_specs=(P("side", "slab", None), P("slab", None), P("slab", None)),
        check_vma=False,
    )
```

```python
import functools
import math

import jax
import jax.numpy as jnp
import ml_dtypes
import numpy as np
from jax import lax
from jax.experimental import pallas as pl
from jax.experimental.pallas import tpu as pltpu
from jax.sharding import PartitionSpec as P

NX = 4096
NZ = 4096
LAGS = 8
NEWTON = 4
STEPS = 2
SLABS = 128
ROWS = 32
LANES = 128
MESH = pl.DeviceIdType.MESH
F32 = jnp.float32
BF16 = jnp.bfloat16
VMEM_BYTES = 56 * 2**20


def high_low(table, axis):
    table = table.astype(np.float32)
    high = table.astype(ml_dtypes.bfloat16)
    low = (table - high.astype(np.float32)).astype(ml_dtypes.bfloat16)
    return np.concatenate([high, low, high], axis=axis)


def complex_matrix(count, sign):
    angle = 2.0 * math.pi / count * (np.outer(np.arange(count), np.arange(count)) % count)
    cos, sin = np.cos(angle), sign * np.sin(angle)
    return np.block([[cos, -sin], [sin, cos]])


def tables():
    forward, inverse = complex_matrix(128, -1.0), complex_matrix(128, 1.0)
    forward_32 = complex_matrix(32, -1.0).reshape(2, 32, 2, 32)
    inverse_32 = complex_matrix(32, 1.0).reshape(2, 32, 2, 32)
    eye = np.eye(8)
    z_first = np.einsum("ajn,xy->ajxny", forward_32[:, :, 0], eye).reshape(512, 256)
    x_second = np.einsum("akcgx,ij->akicgjx", forward_32.reshape(2, 32, 2, 4, 8), eye).reshape(512, 512)
    x_third = np.einsum("axck,ij->axickj", inverse_32, eye).reshape(512, 512)
    z_last = np.einsum("zcgj,xy->zxcgyj", inverse_32[0].reshape(32, 2, 4, 8), eye).reshape(256, 512) / (NX * NZ)
    phase = 2.0 * math.pi / 4096 * np.outer(np.arange(32), np.arange(128))
    twiddle = np.stack([np.cos(phase), np.sin(phase)]).astype(np.float32)
    return dict(
        z_first=high_low(z_first, 1),
        x_second=high_low(x_second, 1),
        x_third=high_low(x_third, 1),
        z_last=high_low(z_last, 1),
        forward_left=high_low(forward, 1),
        inverse_left=high_low(inverse, 1),
        forward_right=high_low(forward.T, 0),
        inverse_right=high_low(inverse.T, 0),
        twiddle=twiddle,
        twiddle_rows=np.repeat(twiddle, 8, axis=1),
    )


def split(value):
    high = value.astype(BF16)
    low = (value - high.astype(F32)).astype(BF16)
    return high, low


def left_product(table, value):
    high, low = split(value)
    stacked = jnp.concatenate([high, high, low], axis=0)
    return jnp.dot(table, stacked, preferred_element_type=F32)


def right_product(value, table):
    high, low = split(value)
    stacked = jnp.concatenate([high, high, low], axis=1)
    return jnp.dot(stacked, table, preferred_element_type=F32)


def left_product_transposed(table, value):
    high, low = split(value)
    stacked = jnp.concatenate([high, high, low], axis=1)
    return lax.dot_general(table, stacked, (((1,), (1,)), ((), ())), preferred_element_type=F32)


def turn(real, imag, cos, sin):
    return real * cos - imag * sin, real * sin + imag * cos


def flat(chunks, chunk):
    return chunks.at[chunk].reshape(SLABS * 8, LANES)


def turned_rows(real, imag):
    return jnp.concatenate([real, imag], axis=1)


def z_forward(field, group, send, t):
    cos, sin = t["twiddle_rows"][0], t["twiddle_rows"][1]
    rows = slice(group * 8, group * 8 + 8)
    column = jnp.concatenate([field[rows, n * 128 : n * 128 + 128] for n in range(32)], axis=0)
    first = left_product(t["z_first"][...], column)
    real, imag = turn(first[:256], first[256:], cos, -sin)
    result = left_product_transposed(t["forward_left"][...], turned_rows(real, imag))
    for part in range(2):
        for chunk in range(2):
            flat(send, chunk)[pl.ds(group * 2 + part, SLABS, stride=8), :] = result[
                part * 128 : part * 128 + 128, chunk * 128 : chunk * 128 + 128
            ]


def fetch(chunks, places):
    return jnp.concatenate(
        [
            jnp.concatenate(
                [flat(chunks, chunk)[pl.ds(group * 2 + part, SLABS, stride=8), :] for chunk, group in places],
                axis=1,
            )
            for part in range(2)
        ],
        axis=0,
    )


def x_stage(received, chunk, t, middle):
    for pair in range(2):
        rows = fetch(received, [(chunk, 2 * pair), (chunk, 2 * pair + 1)]).T
        first = right_product(rows, t["forward_right"][...])
        cos = t["twiddle"][0, pair * 16 : pair * 16 + 16, :].reshape(2, 1, 8, 128)
        sin = t["twiddle"][1, pair * 16 : pair * 16 + 16, :].reshape(2, 1, 8, 128)
        real, imag = turn(
            first[:, :128].reshape(2, 16, 8, 128), first[:, 128:].reshape(2, 16, 8, 128), cos, -sin
        )
        middle[0, 2 * pair : 2 * pair + 2] = real.reshape(2, 128, 128)
        middle[1, 2 * pair : 2 * pair + 2] = imag.reshape(2, 128, 128)


def middle_columns(middle):
    return jnp.concatenate(
        [
            jnp.concatenate(
                [middle[c, g, q * 64 : q * 64 + 64, :] for c in range(2) for g in range(4)], axis=0
            )
            for q in range(2)
        ],
        axis=1,
    )


def past_sums(kernel, history, sums):
    def add(k, carry):
        lanes = pl.ds(pl.multiple_of(k * 128, 128), 128)
        for pair in range(2):
            rows = slice(pair * 16, pair * 16 + 16)
            weights = [kernel[lag, rows, lanes].astype(F32) for lag in range(1, LAGS + 1)]
            for part in range(2):
                past = [history[lag, part, rows, lanes].astype(F32) for lag in range(LAGS)]
                first = weights[0] * past[0]
                for lag in range(1, LAGS):
                    first = first + weights[lag] * past[lag]
                second = weights[1] * past[0]
                for lag in range(2, LAGS):
                    second = second + weights[lag] * past[lag - 1]
                sums[0, part, rows, lanes] = first
                sums[1, part, rows, lanes] = second
        return carry

    lax.fori_loop(0, 32, add, 0)


def spectrum_phase(step, chunk, received, kernel, sums, send, t, middle, wide):
    x_stage(received, chunk, t, middle)
    cos, sin = t["twiddle_rows"][0], t["twiddle_rows"][1]
    wide[...] = left_product(t["x_second"][...], middle_columns(middle))
    rows = slice(chunk * 16, chunk * 16 + 16)

    def convolve(k, carry):
        lanes = pl.ds(pl.multiple_of(k * 128, 128), 128)
        newest = kernel[0, rows, lanes].astype(F32)
        next_newest = kernel[1, rows, lanes].astype(F32)
        for part in range(2):
            place = pl.ds(pl.multiple_of(part * 256 + k * 8, 8), 8)
            fresh = wide[place, :]
            rounded = jnp.concatenate([fresh[:, :128], fresh[:, 128:]], axis=0).astype(BF16).astype(F32)
            total = newest * rounded + sums[step, part, rows, lanes]
            if step + 1 < STEPS:
                sums[step + 1, part, rows, lanes] = sums[step + 1, part, rows, lanes] + next_newest * rounded
            wide[place, :] = jnp.concatenate([total[:8], total[8:]], axis=1)
        return carry

    lax.fori_loop(0, 32, convolve, 0, unroll=2)
    third = left_product(t["x_third"][...], wide[...])
    turned = []
    for q in range(2):
        piece = third[:, q * 128 : q * 128 + 128]
        turned.append(turned_rows(*turn(piece[:256], piece[256:], cos, sin)))
    for pair in range(2):
        places = [slice((2 * pair + g) * 64, (2 * pair + g) * 64 + 64) for g in range(2)]
        ordered = jnp.concatenate([turned[q][place] for place in places for q in range(2)], axis=0)
        result = left_product_transposed(t["inverse_left"][...], ordered)
        for part in range(2):
            for g in range(2):
                flat(send, chunk)[pl.ds((2 * pair + g) * 2 + part, SLABS, stride=8), :] = result[
                    part * 128 : part * 128 + 128, g * 128 : g * 128 + 128
                ]


def z_inverse(received, group, force, t):
    rows = fetch(received, [(0, group), (1, group)]).T
    first = right_product(rows, t["inverse_right"][...])
    cos = t["twiddle"][0].reshape(4, 1, 8, 128)
    sin = t["twiddle"][1].reshape(4, 1, 8, 128)
    real, imag = turn(first[:, :128].reshape(4, 8, 8, 128), first[:, 128:].reshape(4, 8, 8, 128), cos, sin)
    column = jnp.concatenate([real.reshape(256, 128), imag.reshape(256, 128)], axis=0)
    last = left_product(t["z_last"][...], column)
    for n in range(32):
        force[group * 8 : group * 8 + 8, n * 128 : n * 128 + 128] = last[n * 8 : n * 8 + 8]


def friction(group, is_first, impedance, force, other, prestress, strength, state, speed, rate_out):
    eta_first, eta_second = impedance[0], impedance[1]
    eta_total = eta_first + eta_second
    weight_first = eta_second / eta_total
    weight_second = eta_first / eta_total
    eta_joint = eta_first * eta_second / eta_total
    own_weight = jnp.where(is_first, weight_first, weight_second)
    other_weight = jnp.where(is_first, weight_second, weight_first)
    own_scale = jnp.where(is_first, 1.0 / eta_first, -1.0 / eta_second)

    def solve(index, carry):
        at = (slice(group * 8, group * 8 + 8), pl.ds(pl.multiple_of(index * 512, 512), 512))
        own = force[at]
        stress_now = prestress[at]
        normal = strength[at]
        psi = state[at]
        locked = stress_now + (own_weight * own + other_weight * other[at])
        rate = locked / (eta_joint + normal)
        factor = 0.5 * jnp.exp(psi)
        normal_factor = normal * factor
        for _ in range(NEWTON):
            scaled = factor * rate
            root = jnp.sqrt(1.0 + scaled * scaled)
            arc = jnp.log(jnp.abs(scaled) + root)
            arc = jnp.where(scaled < 0.0, -arc, arc)
            misfit = normal * arc + eta_joint * rate - locked
            rate = rate - 0.5 * misfit * root / (normal_factor + eta_joint * root)
        stress = locked - eta_joint * rate
        speed[at] = (stress_now + own - stress) * own_scale
        rate_out[at] = rate
        state[at] = psi + 0.25 * (jnp.exp(-psi) - jnp.abs(rate))
        return carry

    lax.fori_loop(0, 8, solve, 0)


TABLES = (
    "z_first", "forward_left", "twiddle_rows", "forward_right", "twiddle",
    "x_second", "x_third", "inverse_left", "inverse_right", "z_last",
)
FIELDS = ("velocity", "kernel", "history", "prestress", "strength", "state")


def simulate(*refs):
    count = len(TABLES) + len(FIELDS)
    impedance = refs[0]
    outside = refs[1 : 1 + count]
    speed_out, rate_out, state_out = refs[1 + count : 4 + count]
    inside = refs[4 + count : 4 + 2 * count]
    (send, recv, middle, wide, sums, force, other,
     load_sem, own_sem, send_sem, recv_sem, side_send_sem, side_recv_sem) = refs[4 + 2 * count :]
    names = FIELDS[:1] + TABLES[:3] + FIELDS[1:3] + TABLES[3:] + FIELDS[3:]
    t = dict(zip(names, inside))
    me = lax.axis_index("slab")
    side = lax.axis_index("side")
    barrier = pltpu.get_barrier_semaphore()

    def greet(i, carry):
        there = lax.rem(me + i, SLABS)
        pl.semaphore_signal(barrier, inc=1, device_id=(side, there), device_id_type=MESH)
        return carry

    loads = {
        name: pltpu.make_async_copy(outside[k], inside[k], load_sem.at[k]) for k, name in enumerate(names)
    }
    for name in names[:4]:
        loads[name].start()
    pl.semaphore_signal(barrier, inc=1, device_id=(1 - side, me), device_id_type=MESH)
    lax.fori_loop(1, SLABS, greet, 0, unroll=4)

    def need(*wanted):
        for name in wanted:
            loads.pop(name).wait()

    def place(name, where):
        chunk, first, count = name
        return (chunk, where) if count == 4 else (chunk, where, pl.ds(first * 2, count * 2))

    def own(stage, index):
        name = messages[stage][index]
        mine = place(name, me)
        return pltpu.make_async_copy(
            send.at[(stage,) + mine], recv.at[(stage,) + mine], own_sem.at[stage, index]
        )

    def start(stage, index):
        name = messages[stage][index]

        def one(i, carry):
            there = lax.rem(me + i, SLABS)
            pltpu.make_async_remote_copy(
                src_ref=send.at[(stage,) + place(name, there)],
                dst_ref=recv.at[(stage,) + place(name, me)],
                send_sem=send_sem.at[stage, index],
                recv_sem=recv_sem.at[stage, index],
                device_id=(side, there),
                device_id_type=MESH,
            ).start()
            return carry

        lax.fori_loop(1, SLABS, one, 0, unroll=4)
        own(stage, index).start()

    def arrived(stage, index):
        name = messages[stage][index]
        own(stage, index).wait()
        bulk = recv.at[(stage,) + place(name, pl.ds(0, SLABS - 1))]
        pltpu.make_async_copy(bulk, bulk, recv_sem.at[stage, index]).wait()

    def left(stage, index):
        name = messages[stage][index]
        bulk = send.at[(stage,) + place(name, pl.ds(0, SLABS - 1))]
        pltpu.make_async_copy(bulk, bulk, send_sem.at[stage, index]).wait()

    both = slice(None)
    messages = []
    for step in range(STEPS):
        if step == 0:
            messages.append([(0, 0, 4), (1, 0, 4)])
        else:
            messages.append([(both, 0, 1), (0, 1, 1), (0, 2, 1), (0, 3, 1), (1, 1, 3)])
        messages.append([(0, 0, 4), (1, 0, 1), (1, 1, 1), (1, 2, 1), (1, 3, 1)])

    def across(step, rows):
        lines = pl.ds(rows * 8, 8)
        return pltpu.make_async_remote_copy(
            src_ref=force.at[step, lines],
            dst_ref=other.at[step, lines],
            send_sem=side_send_sem.at[step, rows],
            recv_sem=side_recv_sem.at[step, rows],
            device_id=(1 - side, me),
            device_id_type=MESH,
        )

    need(*names[:4])
    for name in names[4:]:
        loads[name].start()
    for group in range(4):
        z_forward(t["velocity"], group, send.at[0], t)
    pl.semaphore_wait(barrier, SLABS)
    start(0, 0)
    start(0, 1)
    need("kernel", "history")
    past_sums(t["kernel"], t["history"], sums)
    need(*tuple(loads))
    for step in range(STEPS):
        there, back = 2 * step, 2 * step + 1
        last = step == STEPS - 1
        final = len(messages[there]) - 1

        def to_force(group):
            arrived(back, 1 + group)
            z_inverse(recv.at[back], group, force.at[step], t)
            across(step, group).start()

        def to_speed(group):
            across(step, group).wait_recv()
            friction(
                group, side == 0, impedance, force.at[step], other.at[step], t["prestress"], t["strength"],
                t["state"], speed_out if last else t["velocity"], rate_out,
            )
            if not last:
                z_forward(t["velocity"], group, send.at[2 * step + 2], t)
                start(2 * step + 2, group)

        for index in range(final):
            arrived(there, index)
        spectrum_phase(step, 0, recv.at[there], t["kernel"], sums, send.at[back], t, middle, wide)
        start(back, 0)
        arrived(there, final)
        spectrum_phase(step, 1, recv.at[there], t["kernel"], sums, send.at[back], t, middle, wide)
        for group in range(4):
            start(back, 1 + group)
        arrived(back, 0)
        for group in range(3):
            to_force(group)
        if last:
            to_force(3)
            to_speed(0)
        else:
            to_speed(0)
            to_force(3)
        for group in range(1, 4):
            to_speed(group)
        if not last:
            start(2 * step + 2, 4)
    state_out[...] = t["state"][...]
    for stage in range(2 * STEPS):
        for index in range(len(messages[stage])):
            left(stage, index)
    for step in range(STEPS):
        for group in range(4):
            across(step, group).wait_send()


def hand_over(*refs):
    for source, target in zip(refs[:3], refs[3:]):
        target[...] = source[...]


def whole(space=pltpu.VMEM):
    return pl.BlockSpec(memory_space=space)


def local(t, velocity, kernel, history, impedance, prestress, strength, fault_state):
    given = dict(
        t,
        velocity=velocity[0], kernel=kernel[0], history=history[0],
        prestress=prestress, strength=strength, state=fault_state,
    )
    names = FIELDS[:1] + TABLES[:3] + FIELDS[1:3] + TABLES[3:] + FIELDS[3:]
    values = [given[name] for name in names]
    field = jax.ShapeDtypeStruct((ROWS, NZ), F32)
    semaphores = pltpu.SemaphoreType.DMA
    results = pl.pallas_call(
        simulate,
        out_shape=(field, field, field),
        in_specs=[whole(pltpu.SMEM)] + [whole(pl.ANY)] * len(values),
        out_specs=(whole(), whole(), whole()),
        scratch_shapes=[pltpu.VMEM(v.shape, v.dtype) for v in values]
        + [
            pltpu.VMEM((2 * STEPS, 2, SLABS, 8, LANES), F32),
            pltpu.VMEM((2 * STEPS, 2, SLABS, 8, LANES), F32),
            pltpu.VMEM((2, 4, 128, LANES), F32),
            pltpu.VMEM((512, 256), F32),
            pltpu.VMEM((STEPS, 2, ROWS, NX), F32),
            pltpu.VMEM((STEPS, ROWS, NZ), F32),
            pltpu.VMEM((STEPS, ROWS, NZ), F32),
            semaphores((len(values),)),
            semaphores((2 * STEPS, 5)),
            semaphores((2 * STEPS, 5)),
            semaphores((2 * STEPS, 5)),
            semaphores((STEPS, 4)),
            semaphores((STEPS, 4)),
        ],
        compiler_params=pltpu.CompilerParams(
            collective_id=0, has_side_effects=True, vmem_limit_bytes=VMEM_BYTES
        ),
        name="simulate",
    )(impedance, *values)
    speed, rate, state = pl.pallas_call(
        hand_over,
        out_shape=(field, field, field),
        in_specs=[whole()] * 3,
        out_specs=(whole(),) * 3,
        compiler_params=pltpu.CompilerParams(vmem_limit_bytes=VMEM_BYTES),
        name="hand_over",
    )(*results)
    return (speed[None], rate, state)


def solution(mesh):
    placed = (
        P("side", "slab", None),
        P("side", None, "slab", None),
        P("side", None, None, "slab", None),
        P(),
        P("slab", None),
        P("slab", None),
        P("slab", None),
    )
    constants = tables()

    def run(*args):
        return local({name: jnp.asarray(value) for name, value in constants.items()}, *args)

    return jax.shard_map(
        run,
        mesh=mesh,
        in_specs=placed,
        out_specs=(P("side", "slab", None), P("slab", None), P("slab", None)),
        check_vma=False,
    )
```

```python
import functools
import math

import jax
import jax.numpy as jnp
import ml_dtypes
import numpy as np
from jax import lax
from jax.experimental import pallas as pl
from jax.experimental.pallas import tpu as pltpu
from jax.sharding import PartitionSpec as P

NX = 4096
NZ = 4096
LAGS = 8
NEWTON = 4
STEPS = 2
SLABS = 128
ROWS = 32
LANES = 128
MESH = pl.DeviceIdType.MESH
F32 = jnp.float32
BF16 = jnp.bfloat16
VMEM_BYTES = 56 * 2**20


def high_low(table, axis):
    table = table.astype(np.float32)
    high = table.astype(ml_dtypes.bfloat16)
    low = (table - high.astype(np.float32)).astype(ml_dtypes.bfloat16)
    return np.concatenate([high, low, high], axis=axis)


def complex_matrix(count, sign):
    angle = 2.0 * math.pi / count * (np.outer(np.arange(count), np.arange(count)) % count)
    cos, sin = np.cos(angle), sign * np.sin(angle)
    return np.block([[cos, -sin], [sin, cos]])


def tables():
    forward, inverse = complex_matrix(128, -1.0), complex_matrix(128, 1.0)
    forward_32 = complex_matrix(32, -1.0).reshape(2, 32, 2, 32)
    inverse_32 = complex_matrix(32, 1.0).reshape(2, 32, 2, 32)
    eye = np.eye(8)
    z_first = np.einsum("ajn,xy->ajxny", forward_32[:, :, 0], eye).reshape(512, 256)
    x_second = np.einsum("akcgx,ij->akicgjx", forward_32.reshape(2, 32, 2, 4, 8), eye).reshape(512, 512)
    x_third = np.einsum("axck,ij->axickj", inverse_32, eye).reshape(512, 512)
    z_last = np.einsum("zcgj,xy->zxcgyj", inverse_32[0].reshape(32, 2, 4, 8), eye).reshape(256, 512) / (NX * NZ)
    phase = 2.0 * math.pi / 4096 * np.outer(np.arange(32), np.arange(128))
    twiddle = np.stack([np.cos(phase), np.sin(phase)]).astype(np.float32)
    return dict(
        z_first=high_low(z_first, 1),
        x_second=high_low(x_second, 1),
        x_third=high_low(x_third, 1),
        z_last=high_low(z_last, 1),
        forward_left=high_low(forward, 1),
        inverse_left=high_low(inverse, 1),
        forward_right=high_low(forward.T, 0),
        inverse_right=high_low(inverse.T, 0),
        twiddle=twiddle,
        twiddle_rows=np.repeat(twiddle, 8, axis=1),
    )


def split(value):
    high = value.astype(BF16)
    low = (value - high.astype(F32)).astype(BF16)
    return high, low


def left_product(table, value):
    high, low = split(value)
    stacked = jnp.concatenate([high, high, low], axis=0)
    return jnp.dot(table, stacked, preferred_element_type=F32)


def right_product(value, table):
    high, low = split(value)
    stacked = jnp.concatenate([high, high, low], axis=1)
    return jnp.dot(stacked, table, preferred_element_type=F32)


def left_product_transposed(table, value):
    high, low = split(value)
    stacked = jnp.concatenate([high, high, low], axis=1)
    return lax.dot_general(table, stacked, (((1,), (1,)), ((), ())), preferred_element_type=F32)


def turn(real, imag, cos, sin):
    return real * cos - imag * sin, real * sin + imag * cos


def flat(chunks, chunk):
    return chunks.at[chunk].reshape(SLABS * 8, LANES)


def turned_rows(real, imag):
    return jnp.concatenate([real, imag], axis=1)


def z_forward(field, group, send, t):
    cos, sin = t["twiddle_rows"][0], t["twiddle_rows"][1]
    rows = slice(group * 8, group * 8 + 8)
    column = jnp.concatenate([field[rows, n * 128 : n * 128 + 128] for n in range(32)], axis=0)
    first = left_product(t["z_first"][...], column)
    real, imag = turn(first[:256], first[256:], cos, -sin)
    result = left_product_transposed(t["forward_left"][...], turned_rows(real, imag))
    for part in range(2):
        for chunk in range(2):
            flat(send, chunk)[pl.ds(group * 2 + part, SLABS, stride=8), :] = result[
                part * 128 : part * 128 + 128, chunk * 128 : chunk * 128 + 128
            ]


def fetch(chunks, places):
    return jnp.concatenate(
        [
            jnp.concatenate(
                [flat(chunks, chunk)[pl.ds(group * 2 + part, SLABS, stride=8), :] for chunk, group in places],
                axis=1,
            )
            for part in range(2)
        ],
        axis=0,
    )


def x_stage(received, chunk, t, middle):
    for pair in range(2):
        rows = fetch(received, [(chunk, 2 * pair), (chunk, 2 * pair + 1)]).T
        first = right_product(rows, t["forward_right"][...])
        cos = t["twiddle"][0, pair * 16 : pair * 16 + 16, :].reshape(2, 1, 8, 128)
        sin = t["twiddle"][1, pair * 16 : pair * 16 + 16, :].reshape(2, 1, 8, 128)
        real, imag = turn(
            first[:, :128].reshape(2, 16, 8, 128), first[:, 128:].reshape(2, 16, 8, 128), cos, -sin
        )
        middle[0, 2 * pair : 2 * pair + 2] = real.reshape(2, 128, 128)
        middle[1, 2 * pair : 2 * pair + 2] = imag.reshape(2, 128, 128)


def middle_columns(middle):
    return jnp.concatenate(
        [
            jnp.concatenate(
                [middle[c, g, q * 64 : q * 64 + 64, :] for c in range(2) for g in range(4)], axis=0
            )
            for q in range(2)
        ],
        axis=1,
    )


def past_sums(kernel, history, sums):
    def add(k, carry):
        lanes = pl.ds(pl.multiple_of(k * 128, 128), 128)
        for pair in range(2):
            rows = slice(pair * 16, pair * 16 + 16)
            weights = [kernel[lag, rows, lanes].astype(F32) for lag in range(1, LAGS + 1)]
            for part in range(2):
                past = [history[lag, part, rows, lanes].astype(F32) for lag in range(LAGS)]
                first = weights[0] * past[0]
                for lag in range(1, LAGS):
                    first = first + weights[lag] * past[lag]
                second = weights[1] * past[0]
                for lag in range(2, LAGS):
                    second = second + weights[lag] * past[lag - 1]
                sums[0, part, rows, lanes] = first
                sums[1, part, rows, lanes] = second
        return carry

    lax.fori_loop(0, 32, add, 0)


def spectrum_phase(step, chunk, received, kernel, sums, send, t, middle, wide):
    x_stage(received, chunk, t, middle)
    cos, sin = t["twiddle_rows"][0], t["twiddle_rows"][1]
    wide[...] = left_product(t["x_second"][...], middle_columns(middle))
    rows = slice(chunk * 16, chunk * 16 + 16)

    def convolve(k, carry):
        lanes = pl.ds(pl.multiple_of(k * 128, 128), 128)
        newest = kernel[0, rows, lanes].astype(F32)
        next_newest = kernel[1, rows, lanes].astype(F32)
        for part in range(2):
            place = pl.ds(pl.multiple_of(part * 256 + k * 8, 8), 8)
            fresh = wide[place, :]
            rounded = jnp.concatenate([fresh[:, :128], fresh[:, 128:]], axis=0).astype(BF16).astype(F32)
            total = newest * rounded + sums[step, part, rows, lanes]
            if step + 1 < STEPS:
                sums[step + 1, part, rows, lanes] = sums[step + 1, part, rows, lanes] + next_newest * rounded
            wide[place, :] = jnp.concatenate([total[:8], total[8:]], axis=1)
        return carry

    lax.fori_loop(0, 32, convolve, 0, unroll=2)
    third = left_product(t["x_third"][...], wide[...])
    turned = []
    for q in range(2):
        piece = third[:, q * 128 : q * 128 + 128]
        turned.append(turned_rows(*turn(piece[:256], piece[256:], cos, sin)))
    for pair in range(2):
        places = [slice((2 * pair + g) * 64, (2 * pair + g) * 64 + 64) for g in range(2)]
        ordered = jnp.concatenate([turned[q][place] for place in places for q in range(2)], axis=0)
        result = left_product_transposed(t["inverse_left"][...], ordered)
        for part in range(2):
            for g in range(2):
                flat(send, chunk)[pl.ds((2 * pair + g) * 2 + part, SLABS, stride=8), :] = result[
                    part * 128 : part * 128 + 128, g * 128 : g * 128 + 128
                ]


def z_inverse(received, group, force, t):
    rows = fetch(received, [(0, group), (1, group)]).T
    first = right_product(rows, t["inverse_right"][...])
    cos = t["twiddle"][0].reshape(4, 1, 8, 128)
    sin = t["twiddle"][1].reshape(4, 1, 8, 128)
    real, imag = turn(first[:, :128].reshape(4, 8, 8, 128), first[:, 128:].reshape(4, 8, 8, 128), cos, sin)
    column = jnp.concatenate([real.reshape(256, 128), imag.reshape(256, 128)], axis=0)
    last = left_product(t["z_last"][...], column)
    for n in range(32):
        force[group * 8 : group * 8 + 8, n * 128 : n * 128 + 128] = last[n * 8 : n * 8 + 8]


def friction(group, is_first, impedance, force, other, prestress, strength, state, speed, rate_out):
    eta_first, eta_second = impedance[0], impedance[1]
    eta_total = eta_first + eta_second
    weight_first = eta_second / eta_total
    weight_second = eta_first / eta_total
    eta_joint = eta_first * eta_second / eta_total
    own_weight = jnp.where(is_first, weight_first, weight_second)
    other_weight = jnp.where(is_first, weight_second, weight_first)
    own_scale = jnp.where(is_first, 1.0 / eta_first, -1.0 / eta_second)

    def solve(index, carry):
        at = (slice(group * 8, group * 8 + 8), pl.ds(pl.multiple_of(index * 512, 512), 512))
        own = force[at]
        stress_now = prestress[at]
        normal = strength[at]
        psi = state[at]
        locked = stress_now + (own_weight * own + other_weight * other[at])
        rate = locked / (eta_joint + normal)
        factor = 0.5 * jnp.exp(psi)
        normal_factor = normal * factor
        for _ in range(NEWTON):
            scaled = factor * rate
            root = jnp.sqrt(1.0 + scaled * scaled)
            arc = jnp.log(jnp.abs(scaled) + root)
            arc = jnp.where(scaled < 0.0, -arc, arc)
            misfit = normal * arc + eta_joint * rate - locked
            rate = rate - 0.5 * misfit * root / (normal_factor + eta_joint * root)
        stress = locked - eta_joint * rate
        speed[at] = (stress_now + own - stress) * own_scale
        rate_out[at] = rate
        state[at] = psi + 0.25 * (jnp.exp(-psi) - jnp.abs(rate))
        return carry

    lax.fori_loop(0, 8, solve, 0)


TABLES = (
    "z_first", "forward_left", "twiddle_rows", "forward_right", "twiddle",
    "x_second", "x_third", "inverse_left", "inverse_right", "z_last",
)
FIELDS = ("velocity", "kernel", "history", "prestress", "strength", "state")


def simulate(*refs):
    count = len(TABLES) + len(FIELDS)
    impedance = refs[0]
    outside = refs[1 : 1 + count]
    speed_out, rate_out, state_out = refs[1 + count : 4 + count]
    inside = refs[4 + count : 4 + 2 * count]
    (send, recv, middle, wide, sums, force, other,
     load_sem, own_sem, send_sem, recv_sem, side_send_sem, side_recv_sem) = refs[4 + 2 * count :]
    names = FIELDS[:1] + TABLES[:3] + FIELDS[1:3] + TABLES[3:] + FIELDS[3:]
    t = dict(zip(names, inside))
    me = lax.axis_index("slab")
    side = lax.axis_index("side")
    barrier = pltpu.get_barrier_semaphore()

    def greet(i, carry):
        there = lax.rem(me + i, SLABS)
        pl.semaphore_signal(barrier, inc=1, device_id=(side, there), device_id_type=MESH)
        return carry

    loads = {
        name: pltpu.make_async_copy(outside[k], inside[k], load_sem.at[k]) for k, name in enumerate(names)
    }
    for name in names[:4]:
        loads[name].start()
    pl.semaphore_signal(barrier, inc=1, device_id=(1 - side, me), device_id_type=MESH)
    lax.fori_loop(1, SLABS, greet, 0, unroll=4)

    def need(*wanted):
        for name in wanted:
            loads.pop(name).wait()

    def place(name, where):
        chunk, first, count = name
        return (chunk, where) if count == 4 else (chunk, where, pl.ds(first * 2, count * 2))

    def own(stage, index):
        name = messages[stage][index]
        mine = place(name, me)
        return pltpu.make_async_copy(
            send.at[(stage,) + mine], recv.at[(stage,) + mine], own_sem.at[stage, index]
        )

    def start(stage, index):
        name = messages[stage][index]

        def one(i, carry):
            there = lax.rem(me + i, SLABS)
            pltpu.make_async_remote_copy(
                src_ref=send.at[(stage,) + place(name, there)],
                dst_ref=recv.at[(stage,) + place(name, me)],
                send_sem=send_sem.at[stage, index],
                recv_sem=recv_sem.at[stage, index],
                device_id=(side, there),
                device_id_type=MESH,
            ).start()
            return carry

        lax.fori_loop(1, SLABS, one, 0, unroll=4)
        own(stage, index).start()

    def arrived(stage, index):
        name = messages[stage][index]
        own(stage, index).wait()
        bulk = recv.at[(stage,) + place(name, pl.ds(0, SLABS - 1))]
        pltpu.make_async_copy(bulk, bulk, recv_sem.at[stage, index]).wait()

    def left(stage, index):
        name = messages[stage][index]
        bulk = send.at[(stage,) + place(name, pl.ds(0, SLABS - 1))]
        pltpu.make_async_copy(bulk, bulk, send_sem.at[stage, index]).wait()

    both = slice(None)
    messages = []
    for step in range(STEPS):
        if step == 0:
            messages.append([(0, 0, 4), (1, 0, 4)])
        else:
            messages.append([(both, 0, 1), (0, 1, 1), (0, 2, 1), (0, 3, 1), (1, 1, 3)])
        messages.append([(0, 0, 3), (1, 0, 1), (1, 1, 1), (1, 2, 1), (both, 3, 1)])

    def across(step, rows):
        lines = pl.ds(rows * 8, 8)
        return pltpu.make_async_remote_copy(
            src_ref=force.at[step, lines],
            dst_ref=other.at[step, lines],
            send_sem=side_send_sem.at[step, rows],
            recv_sem=side_recv_sem.at[step, rows],
            device_id=(1 - side, me),
            device_id_type=MESH,
        )

    need(*names[:4])
    for name in names[4:]:
        loads[name].start()
    for group in range(4):
        z_forward(t["velocity"], group, send.at[0], t)
    pl.semaphore_wait(barrier, SLABS)
    start(0, 0)
    start(0, 1)
    need("kernel", "history")
    past_sums(t["kernel"], t["history"], sums)
    need(*tuple(loads))
    for step in range(STEPS):
        there, back = 2 * step, 2 * step + 1
        last = step == STEPS - 1
        final = len(messages[there]) - 1

        def to_force(group):
            arrived(back, 1 + group)
            z_inverse(recv.at[back], group, force.at[step], t)
            across(step, group).start()

        def to_speed(group):
            across(step, group).wait_recv()
            friction(
                group, side == 0, impedance, force.at[step], other.at[step], t["prestress"], t["strength"],
                t["state"], speed_out if last else t["velocity"], rate_out,
            )
            if not last:
                z_forward(t["velocity"], group, send.at[2 * step + 2], t)
                start(2 * step + 2, group)

        for index in range(final):
            arrived(there, index)
        spectrum_phase(step, 0, recv.at[there], t["kernel"], sums, send.at[back], t, middle, wide)
        start(back, 0)
        arrived(there, final)
        spectrum_phase(step, 1, recv.at[there], t["kernel"], sums, send.at[back], t, middle, wide)
        for group in range(4):
            start(back, 1 + group)
        arrived(back, 0)
        for group in range(3):
            to_force(group)
        if last:
            to_force(3)
            to_speed(0)
        else:
            to_speed(0)
            to_force(3)
        for group in range(1, 4):
            to_speed(group)
        if not last:
            start(2 * step + 2, 4)
    state_out[...] = t["state"][...]
    for stage in range(2 * STEPS):
        for index in range(len(messages[stage])):
            left(stage, index)
    for step in range(STEPS):
        for group in range(4):
            across(step, group).wait_send()


def hand_over(*refs):
    for source, target in zip(refs[:3], refs[3:]):
        target[...] = source[...]


def whole(space=pltpu.VMEM):
    return pl.BlockSpec(memory_space=space)


def local(t, velocity, kernel, history, impedance, prestress, strength, fault_state):
    given = dict(
        t,
        velocity=velocity[0], kernel=kernel[0], history=history[0],
        prestress=prestress, strength=strength, state=fault_state,
    )
    names = FIELDS[:1] + TABLES[:3] + FIELDS[1:3] + TABLES[3:] + FIELDS[3:]
    values = [given[name] for name in names]
    field = jax.ShapeDtypeStruct((ROWS, NZ), F32)
    semaphores = pltpu.SemaphoreType.DMA
    results = pl.pallas_call(
        simulate,
        out_shape=(field, field, field),
        in_specs=[whole(pltpu.SMEM)] + [whole(pl.ANY)] * len(values),
        out_specs=(whole(), whole(), whole()),
        scratch_shapes=[pltpu.VMEM(v.shape, v.dtype) for v in values]
        + [
            pltpu.VMEM((2 * STEPS, 2, SLABS, 8, LANES), F32),
            pltpu.VMEM((2 * STEPS, 2, SLABS, 8, LANES), F32),
            pltpu.VMEM((2, 4, 128, LANES), F32),
            pltpu.VMEM((512, 256), F32),
            pltpu.VMEM((STEPS, 2, ROWS, NX), F32),
            pltpu.VMEM((STEPS, ROWS, NZ), F32),
            pltpu.VMEM((STEPS, ROWS, NZ), F32),
            semaphores((len(values),)),
            semaphores((2 * STEPS, 5)),
            semaphores((2 * STEPS, 5)),
            semaphores((2 * STEPS, 5)),
            semaphores((STEPS, 4)),
            semaphores((STEPS, 4)),
        ],
        compiler_params=pltpu.CompilerParams(
            collective_id=0, has_side_effects=True, vmem_limit_bytes=VMEM_BYTES
        ),
        name="simulate",
    )(impedance, *values)
    speed, rate, state = pl.pallas_call(
        hand_over,
        out_shape=(field, field, field),
        in_specs=[whole()] * 3,
        out_specs=(whole(),) * 3,
        compiler_params=pltpu.CompilerParams(vmem_limit_bytes=VMEM_BYTES),
        name="hand_over",
    )(*results)
    return (speed[None], rate, state)


def solution(mesh):
    placed = (
        P("side", "slab", None),
        P("side", None, "slab", None),
        P("side", None, None, "slab", None),
        P(),
        P("slab", None),
        P("slab", None),
        P("slab", None),
    )
    constants = tables()

    def run(*args):
        return local({name: jnp.asarray(value) for name, value in constants.items()}, *args)

    return jax.shard_map(
        run,
        mesh=mesh,
        in_specs=placed,
        out_specs=(P("side", "slab", None), P("slab", None), P("slab", None)),
        check_vma=False,
    )
```
